32 devices in a mesh: parts: 2 (over y), rep: 4 (over x, core), tp: 4 (over z).
Axes of the slice: x: 2, y: 2, z: 4, core: 2. Of those that a mesh axis runs over, the one named last changes fastest.
Arguments:
- queries: bfloat16 [1024, 8, 128], P(('parts', 'rep'), 'tp'), parts along dimension 0, may hold values from -120 to 120
- fresh_kv: bfloat16 [1024, 8, 2, 128], P(('parts', 'rep'), 'tp'), parts along dimension 0, may hold values from -6 to 6, as said below
- kv_pool: bfloat16 [8960, 8, 2, 16, 128], P(('parts', 'rep'), 'tp'), parts along dimension 0, may hold values from -6 to 6, as said below
- page_table: int32 [1024, 8], P(('parts', 'rep')), parts along dimension 0, may hold values from 0 to 1119, as said below
- lengths: int32 [1024], P(('parts', 'rep')), parts along dimension 0, may hold values from 2 to 128
- mig_src: int32 [8, 4, 32], P(('parts', 'rep')), parts along dimension 0, may hold values from 0 to 1118, as said below
- mig_dst: int32 [8, 4, 32], P(('parts', 'rep')), parts along dimension 0, may hold values from 0 to 1119, as said below
- mig_count: int32 [8, 4], P(('parts', 'rep')), parts along dimension 0, may hold values from 0 to 32, as said below
- residual: bfloat16 [1024, 12288], P(('parts', 'rep'), 'tp'), parts along dimension 0, may hold values from -11 to 11
- out_weight: bfloat16 [1024, 12288], P('tp'), may hold values from -0.5 to 0.5
- norm_gain: bfloat16 [12288], replicated, may hold values from 0.5 to 1.5
Outputs:
- layer_out: bfloat16 [1024, 12288], P(('parts', 'rep'), 'tp'), parts along dimension 0
The draws below stay inside these ranges and needn't reach their ends.
There are 2 independent parts, one for each index of `parts`. The reference program is written for one: setup_inputs(seed, part) draws one part's arguments, and reference() takes and returns one part's arrays. A program takes and returns all parts, laid end to end along the dimension named above; an argument that names none is the same for every part. Nothing has to cross between parts.
Inputs may be any that keep to these rules, and one draw needn't show every extreme that they name: `page_table`: the 8 entries of a row are distinct pages of its replica's pool; rows of one replica share no page. `mig_src`: entries j >= mig_count[d, s] are unused; used entries of one source are distinct pages that no row of its page_table names. `mig_dst`: used entries of one destination are distinct and are pages that its page_table names, whole requests' pages at a time; entries j >= mig_count[d, s] are unused. `mig_count`: A multiple of 8; zero when d equals s. `fresh_kv`: copies c and c2 hold equal numbers when c * 1 equals c2 * 1. `kv_pool`: copies c and c2 hold equal numbers when c * 1 equals c2 * 1.
All inputs are finite; a program needn't handle non-finite values.
Results may differ from the reference program's by a relative error of at most 0.0054.
Values may be sent and summed in bfloat16 or wider, within the bound.
A program may use at most 192 MiB of HBM per device.

```python
from functools import partial
import jax
import jax.numpy as jnp
from jax import lax

D = 12288
HD = 128
KVH = 8
HEAD_DEV = 2
SLOTS = 128
PAGE = 16
MAXP = 8
CAPR = 4
HEADS = 8
KVC = 8
GROUP = 1
CAP = 32
POOL = 1120
REQS = 512
N_REP = 4


def place_page(perm, value, spot):
    where_now = jnp.argmax((perm == value).astype(jnp.int32)).astype(jnp.int32)
    moved = perm.at[where_now].set(perm[spot])
    return moved.at[spot].set(value)


def arrange_pool(perm, first_slot):
    perm = place_page(perm, 0, first_slot * MAXP)
    perm = place_page(perm, POOL - 1, first_slot * MAXP + 1)
    return place_page(perm, POOL - 2, SLOTS * MAXP)


def draw_tables(key):
    rep_index = jnp.arange(N_REP, dtype=jnp.int32)
    order_keys = jax.random.split(jax.random.fold_in(key, 102), N_REP)
    orders = jax.vmap(lambda single: jax.random.permutation(single, SLOTS))(order_keys).astype(jnp.int32)
    perm_keys = jax.random.split(jax.random.fold_in(key, 101), N_REP)
    perms = jax.vmap(lambda single: jax.random.permutation(single, POOL))(perm_keys).astype(jnp.int32)
    perms = jax.vmap(arrange_pool)(perms, orders[:, 0]).astype(jnp.int32)
    counts = jax.random.randint(jax.random.fold_in(key, 103), (N_REP, N_REP), 1, CAPR + 1).astype(jnp.int32)
    counts = jnp.where(rep_index[:, None] == rep_index[None, :], 0, counts)
    counts = counts.at[N_REP - 1, 0].set(CAPR)
    table = perms[:, :SLOTS * MAXP].reshape(N_REP * SLOTS, MAXP)
    before_dest = jnp.cumsum(counts, axis=1) - counts
    before_source = jnp.cumsum(counts, axis=0) - counts
    item_index = jnp.arange(CAPR, dtype=jnp.int32)
    valid = item_index[None, None, :] < counts[:, :, None]
    page_index = jnp.arange(MAXP, dtype=jnp.int32)
    out_index = jnp.where(valid, before_dest[:, :, None] + item_index, 0)
    src_pos = SLOTS * MAXP + out_index[..., None] * MAXP + page_index
    src_pages = perms[rep_index[:, None, None, None], src_pos]
    src_pages = jnp.where(valid[..., None], src_pages, 0).reshape(N_REP, N_REP, CAP)
    in_index = jnp.where(valid, before_source[:, :, None] + item_index, 0)
    dest_slot = orders[rep_index[None, :, None], in_index]
    dst_pages = perms[rep_index[None, :, None, None], dest_slot[..., None] * MAXP + page_index]
    dst_pages = jnp.where(valid[..., None], dst_pages, 0).reshape(N_REP, N_REP, CAP)
    dst_pages = jnp.transpose(dst_pages, (1, 0, 2))
    page_counts = jnp.transpose(counts) * MAXP
    limits = 2 + (MAXP * PAGE - 2) * (rep_index + 1) // N_REP
    seq_lengths = jax.random.randint(jax.random.fold_in(key, 104), (N_REP, SLOTS), 2, limits[:, None] + 1)
    seq_lengths = seq_lengths.reshape(N_REP * SLOTS).astype(jnp.int32)
    seq_lengths = seq_lengths.at[(N_REP - 1) * SLOTS].set(MAXP * PAGE)
    seq_lengths = seq_lengths.at[0].set(2)
    return (table, seq_lengths, src_pages.astype(jnp.int32), dst_pages.astype(jnp.int32), page_counts.astype(jnp.int32))


def pool_normals(key):
    drawn = jax.random.normal(jax.random.fold_in(key, 201), (N_REP * POOL, KVH, 2, PAGE, HD), jnp.float32)
    return jnp.clip(drawn, -6.0, 6.0)


def draw_page_table(key, part):
    shared = draw_tables(key)
    return shared[0]


def draw_lengths(key, part):
    shared = draw_tables(key)
    return shared[1]


def draw_mig_src(key, part):
    shared = draw_tables(key)
    return shared[2]


def draw_mig_dst(key, part):
    shared = draw_tables(key)
    return shared[3]


def draw_mig_count(key, part):
    shared = draw_tables(key)
    return shared[4]


def draw_kv_pool(key, part):
    normals = pool_normals(key)
    return jnp.repeat(normals, KVC // KVH, axis=1).astype(jnp.bfloat16)


def draw_queries(key, part):
    key = jax.random.fold_in(key, 3)
    values_drawn = jnp.clip(jax.random.normal(key, (REQS, HEADS, HD), jnp.float32), -6.0, 6.0)
    return values_drawn.astype(jnp.bfloat16)


def draw_fresh_kv(key, part):
    key = jax.random.fold_in(key, 4)
    values_drawn = jnp.clip(jax.random.normal(key, (REQS, KVH, 2, HD), jnp.float32), -6.0, 6.0)
    return jnp.repeat(values_drawn, KVC // KVH, axis=1).astype(jnp.bfloat16)


def draw_residual(key, part):
    key = jax.random.fold_in(key, 5)
    ramp = 0.25 + 0.5 * jnp.arange(D, dtype=jnp.float32) / D
    values_drawn = jnp.clip(jax.random.normal(key, (REQS, D), jnp.float32), -6.0, 6.0)
    return (values_drawn * ramp).astype(jnp.bfloat16)


def with_spikes(entries, key, source, target, blocks, factor):
    def block_of(position):
        return (jnp.arange(entries.shape[position]) // (entries.shape[position] // blocks)).reshape((-1,) + (1,) * (entries.ndim - 1 - position))

    first = jax.random.permutation(key, blocks)[block_of(target)]
    far = (block_of(target) + blocks // 2) % blocks
    return jnp.where((block_of(source) == first) | (block_of(source) == far), factor * entries, entries)


def steps_of(own_key, shape, cuts, smallest, largest):
    def one(dim, shards_of):
        steps = jax.random.uniform(jax.random.fold_in(jax.random.fold_in(own_key, 6), dim), (shards_of,), jnp.float32, smallest / len(cuts), largest / len(cuts))
        return jnp.repeat(jnp.exp(steps), shape[dim] // shards_of).reshape((-1,) + (1,) * (len(shape) - dim - 1))

    gain = one(*cuts[0])
    for cut in cuts[1:]:
        gain = gain * one(*cut)
    return gain


def gaussian_with(own_key, extent, width, most, shards, heavy, kind=jnp.bfloat16):
    values = width * jax.random.normal(own_key, extent, jnp.float32)
    if shards:
        values = values * steps_of(own_key, extent, shards, -0.22, 0.18)
    return jnp.clip(with_spikes(values, jax.random.fold_in(own_key, 3), *heavy), -most, most).astype(kind)


def setup_inputs(seed: int = 0, part: int = 0) -> dict:
    key_list = jax.random.split(jax.random.key(seed), 12)
    part_splits = jax.random.split(jax.random.fold_in(key_list[11], part), 12)
    return {
        "queries": draw_queries(jax.random.fold_in(jax.random.fold_in(key_list[11], part), 71), part),
        "fresh_kv": draw_fresh_kv(jax.random.fold_in(jax.random.fold_in(key_list[11], part), 71), part),
        "kv_pool": draw_kv_pool(jax.random.fold_in(jax.random.fold_in(key_list[11], part), 71), part),
        "page_table": draw_page_table(jax.random.fold_in(jax.random.fold_in(key_list[11], part), 71), part),
        "lengths": draw_lengths(jax.random.fold_in(jax.random.fold_in(key_list[11], part), 71), part),
        "mig_src": draw_mig_src(jax.random.fold_in(jax.random.fold_in(key_list[11], part), 71), part),
        "mig_dst": draw_mig_dst(jax.random.fold_in(jax.random.fold_in(key_list[11], part), 71), part),
        "mig_count": draw_mig_count(jax.random.fold_in(jax.random.fold_in(key_list[11], part), 71), part),
        "residual": draw_residual(jax.random.fold_in(jax.random.fold_in(key_list[11], part), 71), part),
        "out_weight": gaussian_with(key_list[9], (HEADS * HD, D), (HEAD_DEV * HD) ** -0.5, 0.5, ((0, 4),), (0, 1, 4, 2.0)),
        "norm_gain": jnp.clip(1.0 + 0.1 * jax.random.normal(key_list[10], (D,), jnp.float32), 0.5, 1.5).astype(jnp.bfloat16),
    }


EPSILON = 1e-05

def migrate(kv_pool, mig_src, mig_dst, mig_count):
    replica_pools = kv_pool.reshape((N_REP, POOL) + kv_pool.shape[1:])
    positions = jnp.arange(CAP, dtype=jnp.int32)
    updated = []
    for target in range(N_REP):
        current = replica_pools[target]
        for source in range(N_REP):
            moving = replica_pools[source][mig_src[source, target]]
            places = jnp.where(positions < mig_count[target, source], mig_dst[target, source], POOL)
            current = current.at[places].set(moving, mode='drop')
        updated.append(current)
    return jnp.stack(updated).reshape(kv_pool.shape)

def attend_row(flat_pool, row_input):
    table_row, seq_length, query_row, fresh_row = row_input
    page_blocks = flat_pool[table_row].astype(jnp.float32)
    key_blocks = page_blocks[:, :, 0]
    value_blocks = page_blocks[:, :, 1]
    query_float = query_row.reshape(KVC, GROUP, HD).astype(jnp.float32)
    fresh_float = fresh_row.astype(jnp.float32)
    scaling = HD ** (-0.5)
    scores = jnp.einsum('cgd,mcpd->cgmp', query_float, key_blocks).reshape(KVC, GROUP, MAXP * PAGE) * scaling
    self_score = jnp.einsum('cgd,cd->cg', query_float, fresh_float[:, 0]) * scaling
    live_mask = jnp.arange(MAXP * PAGE, dtype=jnp.int32) < seq_length
    scores = jnp.where(live_mask, scores, -jnp.inf)
    highest = jnp.maximum(lax.optimization_barrier(jnp.max(scores, axis=2)), self_score)
    cache_mass = jnp.exp(scores - highest[..., None])
    self_mass = jnp.exp(self_score - highest)
    total_mass = lax.optimization_barrier(jnp.sum(cache_mass, axis=2)) + self_mass
    weights = (cache_mass / total_mass[..., None]).astype(jnp.bfloat16)
    self_weight = (self_mass / total_mass).astype(jnp.bfloat16)
    context = jnp.einsum('cgmp,mcpd->cgd', weights.reshape(KVC, GROUP, MAXP, PAGE).astype(jnp.float32), value_blocks)
    context = context + self_weight.astype(jnp.float32)[..., None] * fresh_float[:, 1][:, None, :]
    return context.reshape(HEADS * HD).astype(jnp.bfloat16)

def reference(queries, fresh_kv, kv_pool, page_table, lengths, mig_src, mig_dst, mig_count, residual, out_weight, norm_gain):
    moved_pool = migrate(kv_pool, mig_src, mig_dst, mig_count)
    offsets = jnp.arange(REQS, dtype=jnp.int32) // SLOTS * POOL
    global_table = (page_table + offsets[:, None]).astype(jnp.int32)
    attended = lax.map(partial(attend_row, moved_pool), (global_table, lengths, queries, fresh_kv))
    summed = jnp.dot(attended, out_weight, preferred_element_type=jnp.float32) + residual.astype(jnp.float32)
    mean_square = lax.optimization_barrier(jnp.mean(summed * summed, axis=1, keepdims=True))
    return (norm_gain.astype(jnp.float32) * summed * lax.rsqrt(mean_square + EPSILON)).astype(jnp.bfloat16)
```

```python
import functools
import math

import jax
import jax.numpy as jnp
import numpy as np
from jax import lax
from jax.experimental import pallas as pl
from jax.experimental.pallas import tpu as pltpu
from jax.sharding import PartitionSpec as P

EPSILON = 1e-05
NEVER = -1e30


def attend_kernel(
    rows, group, page_size, step_pages, factor,
    query_ref, fresh_ref, table_ref, code_ref, spread_ref, pool_ref, out_ref, top_ref, mass_ref, sum_ref,
):
    step = pl.program_id(0)
    copies = query_ref.shape[0]
    width = query_ref.shape[2]
    tokens = step_pages * page_size

    @pl.when(step == 0)
    def _():
        for c in range(copies):
            fresh_key = fresh_ref[c, 0].astype(jnp.float32)
            fresh_value = fresh_ref[c, 1].astype(jnp.float32)
            for g in range(group):
                part = slice(g * rows, (g + 1) * rows)
                own = jnp.sum(query_ref[c, part].astype(jnp.float32) * fresh_key, axis=1, keepdims=True)
                top_ref[c, part] = jnp.broadcast_to(own, (rows, width))
                mass_ref[c, part] = jnp.ones((rows, width), jnp.float32)
                sum_ref[c, part] = fresh_value

    page = lax.broadcasted_iota(jnp.int32, (rows, step_pages), 1) + step * step_pages
    found = jnp.zeros((rows, step_pages), jnp.float32)
    for m in range(table_ref.shape[1]):
        found = found + jnp.where(table_ref[:, m : m + 1] == page, code_ref[:, m : m + 1], 0.0)
    code = jnp.sum(found, axis=0, keepdims=True)
    owner = jnp.floor(code * (1.0 / 32.0))
    live = code - 32.0 * owner
    which = lax.broadcasted_iota(jnp.int32, (16, step_pages), 0)
    both = jnp.where(which == 0, owner, live).astype(jnp.bfloat16)
    spread = jnp.dot(both, spread_ref[...], preferred_element_type=jnp.float32)
    position = lax.broadcasted_iota(jnp.int32, (1, tokens), 1) % page_size
    token_owner = jnp.where(position.astype(jnp.float32) < spread[1:2], spread[0:1], -1.0)

    row_id = lax.broadcasted_iota(jnp.int32, (group * rows, 1), 0)
    row_id = (row_id % rows).astype(jnp.float32)
    for c in range(copies):
        keys = pool_ref[:, c, 0].reshape(tokens, width)
        values = pool_ref[:, c, 1].reshape(tokens, width)
        scores = lax.dot_general(
            query_ref[c], keys, (((1,), (1,)), ((), ())), preferred_element_type=jnp.float32
        )
        scores = jnp.where(token_owner == row_id, scores, NEVER)
        before = top_ref[c, :, 0:1]
        highest = jnp.maximum(before, jnp.max(scores, axis=1, keepdims=True))
        decay = jnp.exp2((before - highest) * factor)
        weights = jnp.exp2((scores - highest) * factor)
        mass = jnp.sum(weights, axis=1, keepdims=True)
        context = jnp.dot(weights.astype(jnp.bfloat16), values, preferred_element_type=jnp.float32)
        top_ref[c] = jnp.broadcast_to(highest, top_ref.shape[1:])
        mass_ref[c] = mass_ref[c] * decay + mass
        sum_ref[c] = sum_ref[c] * decay + context

    @pl.when(step == pl.num_programs(0) - 1)
    def _():
        out_ref[...] = (sum_ref[...] / mass_ref[...]).astype(out_ref.dtype)


def attend(query, fresh, table, code, pool, rows):
    copies, total, width = query.shape
    pages, _, _, page_size, _ = pool.shape
    step_pages = next(n for n in (112, 128, 64, 32, 16, 8, 1) if pages % n == 0)
    tokens = step_pages * page_size
    spread = jnp.asarray(np.arange(tokens)[None, :] // page_size == np.arange(step_pages)[:, None], jnp.bfloat16)
    factor = width ** (-0.5) * math.log2(math.e)

    def fixed(array):
        return pl.BlockSpec(array.shape, lambda i, n=array.ndim: (0,) * n)

    return pl.pallas_call(
        functools.partial(attend_kernel, rows, total // rows, page_size, step_pages, factor),
        grid=(pages // step_pages,),
        in_specs=[fixed(a) for a in (query, fresh, table, code, spread)]
        + [pl.BlockSpec((step_pages,) + pool.shape[1:], lambda i: (i, 0, 0, 0, 0))],
        out_specs=fixed(query),
        out_shape=jax.ShapeDtypeStruct(query.shape, query.dtype),
        scratch_shapes=[pltpu.VMEM(query.shape, jnp.float32) for _ in range(3)],
        compiler_params=pltpu.CompilerParams(vmem_limit_bytes=48 * 2**20),
    )(query, fresh, table, code, spread, pool)


def on_device(
    queries, fresh_kv, kv_pool, page_table, lengths, mig_src, mig_dst, mig_count, residual, out_weight, norm_gain,
):
    tp_ranks = lax.axis_size("tp")
    slots, heads, width = queries.shape
    pages, copies, _, page_size, _ = kv_pool.shape
    group = heads // copies
    per_row = page_table.shape[1]
    ranks, capacity = mig_src.shape[1:]
    moves = capacity // per_row
    extra = ranks * moves
    rows = slots + extra

    listed = mig_dst[0].reshape(extra, per_row)
    used = (jnp.arange(moves)[None, :] * per_row < mig_count[0][:, None]).reshape(extra)
    same = listed[:, :, None, None] == page_table[None, None]
    place = jnp.sum(same * jnp.arange(per_row, dtype=jnp.int32), axis=(2, 3))
    chosen = jnp.any(same[:, 0], axis=2) & used[:, None]
    length = jnp.sum(chosen * lengths[None, :], axis=1)
    filled = jnp.clip(length[:, None] - place * page_size, 0, page_size)
    away = jnp.any(chosen, axis=0)
    pick = chosen.astype(jnp.bfloat16)
    query_rows = queries.reshape(slots, heads * width)
    fresh_rows = fresh_kv.reshape(slots, copies * 2 * width)
    payload = jnp.dot(pick, jnp.concatenate([query_rows, fresh_rows], axis=1), preferred_element_type=jnp.float32)
    payload = jnp.concatenate(
        [payload.astype(jnp.bfloat16), jnp.pad(filled, ((0, 0), (0, width - per_row))).astype(jnp.bfloat16)], axis=1
    )
    guest = lax.all_to_all(payload.reshape(ranks, moves, -1), "rep", split_axis=0, concat_axis=0, tiled=True)
    guest = guest.reshape(extra, -1)
    cut = heads * width
    query_all = jnp.concatenate([query_rows, guest[:, :cut]], axis=0)
    fresh_all = jnp.concatenate([fresh_rows, guest[:, cut : cut + copies * 2 * width]], axis=0)
    guest_filled = guest[:, cut + copies * 2 * width :][:, :per_row].astype(jnp.int32)
    table = jnp.concatenate([page_table, mig_src[0].reshape(extra, per_row)], axis=0)
    local = jnp.clip(
        lengths[:, None] - jnp.arange(per_row, dtype=jnp.int32)[None, :] * page_size, 0, page_size
    )
    local = jnp.where(away[:, None], 0, local)
    filled_all = jnp.concatenate([local, guest_filled], axis=0)
    table = jnp.where(filled_all > 0, table, -1)
    code = (jnp.arange(rows, dtype=jnp.int32)[:, None] * 32 + filled_all).astype(jnp.float32)
    query_all = query_all.reshape(rows, copies, group, width).transpose(1, 2, 0, 3).reshape(copies, group * rows, width)
    fresh_all = fresh_all.reshape(rows, copies, 2, width).transpose(1, 2, 0, 3)
    attended = attend(query_all, fresh_all, table, code, kv_pool, rows)
    attended = attended.reshape(copies, group, rows, width).transpose(2, 0, 1, 3).reshape(rows, heads * width)
    back = lax.all_to_all(attended[slots:].reshape(ranks, moves, -1), "rep", split_axis=0, concat_axis=0, tiled=True)
    home = lax.dot_general(
        pick, back.reshape(extra, -1), (((0,), (0,)), ((), ())), preferred_element_type=jnp.float32
    ).astype(jnp.bfloat16)
    attended = jnp.where(away[:, None], home, attended[:slots])

    model_width = out_weight.shape[1]
    local_width = model_width // tp_ranks
    feature_share = lax.psum_scatter(
        lax.dot_general(
            out_weight, attended, (((0,), (1,)), ((), ())), preferred_element_type=jnp.float32
        ),
        "tp",
        scatter_dimension=0,
        tiled=True,
    )
    mixed_out = feature_share.T + residual.astype(jnp.float32)
    squares = lax.psum(jnp.sum(mixed_out * mixed_out, axis=1), "tp")
    scaled = mixed_out * lax.rsqrt(squares / model_width + EPSILON)[:, None]
    local_gain = lax.dynamic_slice_in_dim(
        norm_gain, lax.axis_index("tp") * local_width, local_width, 0
    )
    return (local_gain.astype(jnp.float32)[None, :] * scaled).astype(jnp.bfloat16)


def solution(mesh):
    in_specs = (
        P(("parts", "rep"), "tp", None),
        P(("parts", "rep"), "tp", None, None),
        P(("parts", "rep"), "tp", None, None, None),
        P(("parts", "rep"), None),
        P(("parts", "rep")),
        P(("parts", "rep"), None, None),
        P(("parts", "rep"), None, None),
        P(("parts", "rep"), None),
        P(("parts", "rep"), "tp"),
        P("tp", None),
        P(),
    )
    out_specs = P(("parts", "rep"), "tp")
    return jax.shard_map(
        on_device, mesh=mesh, in_specs=in_specs, out_specs=out_specs, check_vma=False
    )
```

```python
import functools
import math

import jax
import jax.numpy as jnp
from jax import lax
from jax.experimental import pallas as pl
from jax.experimental.pallas import tpu as pltpu
from jax.sharding import PartitionSpec as P

EPSILON = 1e-05
NEVER = -1e30
MESH = pl.DeviceIdType.MESH
TILE = 8


def iota(shape, dimension):
    return lax.broadcasted_iota(jnp.int32, shape, dimension)


def exact_dot(left, right, contract):
    return lax.dot_general(
        left.astype(jnp.bfloat16), right.astype(jnp.bfloat16), (contract, ((), ())), preferred_element_type=jnp.float32
    )


def layer_kernel(
    ranks, tp, copies, group, step_pages, factor,
    inputs_ref, small_ref, table_ref, gain_ref, pool_hbm, residual_hbm, weight_hbm,
    out_ref,
    pool_ref, weight_ref, residual_ref, total_ref, spread_ref, query_ref, fresh_ref, place_ref, code_ref,
    top_ref, mass_ref, sum_ref, ask_ref, asked_ref, reply_ref, replied_ref, gathered_ref, square_ref, squares_ref,
    local_sem, pool_sem, ask_sem, reply_sem, gather_sem, square_sem, weight_send, weight_recv,
):
    slots, per_row = table_ref.shape
    pages, _, _, page_size, width = pool_hbm.shape
    steps = pages // step_pages
    tokens = step_pages * page_size
    heads = copies * group
    entries = small_ref.shape[1]
    capacity = entries // ranks
    moves = capacity // per_row
    extra = ranks * moves
    rows = slots + extra
    padded = ranks * TILE
    depth, local_width = weight_ref.shape[1:]
    segment = depth // (2 * ranks)
    half = segment // 2

    part = lax.axis_index("parts")
    me = lax.axis_index("rep")
    rank = lax.axis_index("tp")
    across_part = 1 - part
    across_rep = lax.rem(me + 2, ranks)
    mate = me + 1 - 2 * lax.rem(me, 2)

    def pool_copy(i):
        spot = pl.ds(i * step_pages, step_pages)
        return pltpu.make_async_copy(pool_hbm.at[spot], pool_ref.at[spot], pool_sem.at[i])

    def peer_rep(k):
        return lax.rem(me + k, ranks)

    def peer_tp(k):
        return lax.rem(rank + k, tp)

    def from_tp(k):
        return lax.rem(rank + tp - k, tp)

    def remote(src, dst, send, recv, **where):
        return pltpu.make_async_remote_copy(
            src_ref=src, dst_ref=dst, send_sem=send, recv_sem=recv, device_id=where, device_id_type=MESH
        )

    barrier = pltpu.get_barrier_semaphore()
    for k in range(1, ranks):
        pl.semaphore_signal(barrier, inc=1, device_id={"rep": peer_rep(k)}, device_id_type=MESH)

    def greet(k, _):
        pl.semaphore_signal(barrier, inc=1, device_id={"tp": peer_tp(k)}, device_id_type=MESH)
        return 0

    lax.fori_loop(1, tp, greet, 0)
    pl.semaphore_signal(barrier, inc=1, device_id={"parts": across_part}, device_id_type=MESH)

    pool_copy(0).start()
    pool_copy(1).start()

    target = small_ref[0:1, :]
    source = small_ref[1:2, :]
    count = small_ref[2:3, :]
    length = small_ref[3:4, :]
    valid = lax.rem(iota((1, entries), 1), capacity) < count
    listed = jnp.zeros((slots, entries), jnp.float32)
    spot_sum = jnp.zeros((slots, entries), jnp.float32)
    for m in range(per_row):
        same = jnp.where((table_ref[:, m : m + 1] == target) & valid, 1.0, 0.0)
        listed = listed + same
        spot_sum = spot_sum + float(m) * same
    length_row = length[:, :slots].astype(jnp.float32)
    diagonal = iota((slots, slots), 0) == iota((slots, slots), 1)
    length_column = jnp.sum(jnp.where(diagonal, length_row, 0.0), axis=1, keepdims=True)
    spot = jnp.sum(spot_sum, axis=0, keepdims=True)
    entry_length = jnp.sum(listed * length_column, axis=0, keepdims=True)
    filled = jnp.clip(entry_length - page_size * spot, 0.0, float(page_size))
    away = jnp.max(listed, axis=1, keepdims=True)
    row = iota((padded, entries), 0)
    column = iota((padded, entries), 1)
    first = row // TILE * capacity + lax.rem(row, TILE) * per_row
    real = lax.rem(row, TILE) < moves
    head_entry = jnp.where((column == first) & real, 1.0, 0.0)
    pick = exact_dot(head_entry, listed, ((1,), (1,)))
    asking = exact_dot(pick, inputs_ref[...], ((1,), (0,)))
    within = jnp.where((column >= first) & (column < first + per_row) & real, filled, 0.0)
    fold = jnp.where(lax.rem(iota((entries, width), 0), per_row) == iota((entries, width), 1), 1.0, 0.0)
    asking_filled = exact_dot(within, fold, ((1,), (0,)))
    asked_width = inputs_ref.shape[1]
    for d in range(ranks):
        ask_ref[d, :, :asked_width] = asking[d * TILE : (d + 1) * TILE]
        ask_ref[d, :, asked_width:] = asking_filled[d * TILE : (d + 1) * TILE]

    pl.semaphore_wait(barrier, ranks + tp - 1)

    def ask(k):
        return remote(ask_ref.at[peer_rep(k)], asked_ref.at[me], ask_sem.at[0, k], ask_sem.at[1, k], rep=peer_rep(k))

    for k in range(1, ranks):
        ask(k).start()

    mine = part * ranks + me

    def piece(t, owner_part, owner_rep, start=0, size=segment):
        begin = pl.multiple_of((owner_part * ranks + owner_rep) * segment + start, half)
        return weight_ref.at[t, pl.ds(begin, size)]

    def hop(kind, k, spot_ref, **where):
        return remote(spot_ref, spot_ref, weight_send.at[kind, k], weight_recv.at[kind, k], **where)

    def spread_first(k):
        other = peer_tp(k)
        begin = pl.multiple_of(mine * segment, segment)
        columns = pl.ds(pl.multiple_of(other * local_width, 128), local_width)
        return remote(
            weight_hbm.at[pl.ds(begin, segment), columns], piece(rank, part, me),
            weight_send.at[0, k], weight_recv.at[0, k], tp=other,
        )

    def own_first(k):
        return hop(1, k, piece(from_tp(k), part, me), rep=across_rep)

    def own_second(k):
        return hop(2, k, piece(from_tp(k), part, me), parts=across_part)

    def own_mate(k):
        return hop(3, k, piece(from_tp(k), part, me), rep=mate)

    def pass_first(k):
        return hop(4, k, piece(from_tp(k), part, across_rep, 0, half), parts=across_part)

    def pass_second(k):
        return hop(5, k, piece(from_tp(k), across_part, me, half, half), rep=across_rep)

    def first_mate(k):
        return hop(6, k, piece(from_tp(k), part, across_rep), rep=mate)

    def second_mate(k):
        return hop(7, k, piece(from_tp(k), across_part, me), rep=mate)

    def corner_mate(k):
        return hop(8, k, piece(from_tp(k), across_part, across_rep), rep=mate)

    def arrival(kind, k, spot_ref):
        hop(kind, k, spot_ref, rep=mate).wait_recv()

    def loop(low, high, body):
        def run(k, _):
            body(k)
            return 0

        lax.fori_loop(low, high, run, 0)

    def stage_one(k):
        arrival(0, k, piece(from_tp(k), part, me))
        own_first(k).start()
        own_second(k).start()
        own_mate(k).start()

    def stage_two(k):
        arrival(1, k, piece(from_tp(k), part, across_rep))
        arrival(2, k, piece(from_tp(k), across_part, me))
        pass_first(k).start()
        pass_second(k).start()
        first_mate(k).start()
        second_mate(k).start()

    def stage_three(k):
        arrival(4, k, piece(from_tp(k), across_part, across_rep, 0, half))
        arrival(5, k, piece(from_tp(k), across_part, across_rep, half, half))
        corner_mate(k).start()

    def stage_end(k):
        mate_rep = lax.rem(mate + 2, ranks)
        arrival(3, k, piece(from_tp(k), part, mate))
        arrival(6, k, piece(from_tp(k), part, mate_rep))
        arrival(7, k, piece(from_tp(k), across_part, mate))
        arrival(8, k, piece(from_tp(k), across_part, mate_rep))
        for copy in (
            spread_first, own_first, own_second, own_mate, pass_first, pass_second, first_mate, second_mate, corner_mate,
        ):
            copy(k).wait_send()

    loop(1, tp, lambda k: spread_first(k).start())

    for i in range(2, steps):
        pool_copy(i).start()
    own_columns = pl.ds(pl.multiple_of(rank * local_width, 128), local_width)
    own_weight = pltpu.make_async_copy(weight_hbm.at[:, own_columns], weight_ref.at[rank], local_sem.at[0])
    own_weight.start()
    load_residual = pltpu.make_async_copy(residual_hbm, residual_ref, local_sem.at[1])
    load_residual.start()

    spread_ref[...] = jnp.where(
        iota((step_pages, tokens), 1) // page_size == iota((step_pages, tokens), 0), 1.0, 0.0
    ).astype(jnp.bfloat16)
    local_filled = jnp.clip(length_column - float(page_size) * iota((slots, per_row), 1).astype(jnp.float32), 0.0, float(page_size))
    local_filled = local_filled * (1.0 - away)
    place_ref[:slots, :] = table_ref[...]
    code_ref[:slots, :] = jnp.where(
        local_filled > 0.0, iota((slots, per_row), 0).astype(jnp.float32) * 32.0 + local_filled, 0.0
    )
    lanes = iota((extra, entries), 1)
    order = iota((extra, entries), 0)
    for m in range(per_row):
        found = jnp.where(lanes == order * per_row + m, source.astype(jnp.float32), 0.0)
        place_ref[slots:, m : m + 1] = jnp.sum(found, axis=1, keepdims=True).astype(jnp.int32)
    for h in range(heads):
        c, g = h // group, h % group
        query_ref[c, g * rows : g * rows + slots] = inputs_ref[:, h * width : (h + 1) * width]
    for c in range(copies):
        for i in range(2):
            begin = (heads + 2 * c + i) * width
            fresh_ref[c, i, :slots] = inputs_ref[:, begin : begin + width]

    asked_ref[pl.ds(me, 1)] = jnp.zeros((1,) + asked_ref.shape[1:], jnp.float32)
    for k in range(1, ranks):
        come = lax.rem(me + ranks - k, ranks)
        remote(asked_ref.at[come], asked_ref.at[come], ask_sem.at[0, k], ask_sem.at[1, k], rep=come).wait_recv()
    asked = asked_ref[...].reshape(padded, asked_ref.shape[2])
    row = iota((extra, padded), 0)
    pack = jnp.where(iota((extra, padded), 1) == row // moves * TILE + lax.rem(row, moves), 1.0, 0.0)
    guests = exact_dot(pack, asked, ((1,), (0,)))
    for h in range(heads):
        c, g = h // group, h % group
        query_ref[c, g * rows + slots : (g + 1) * rows] = guests[:, h * width : (h + 1) * width].astype(jnp.bfloat16)
    for c in range(copies):
        for i in range(2):
            begin = (heads + 2 * c + i) * width
            fresh_ref[c, i, slots:] = guests[:, begin : begin + width].astype(jnp.bfloat16)
    guest_filled = guests[:, asked_width : asked_width + per_row]
    code_ref[slots:, :] = jnp.where(
        guest_filled > 0.0, (iota((extra, per_row), 0) + slots).astype(jnp.float32) * 32.0 + guest_filled, 0.0
    )

    for c in range(copies):
        fresh_key = fresh_ref[c, 0].astype(jnp.float32)
        fresh_value = fresh_ref[c, 1].astype(jnp.float32)
        for g in range(group):
            span = slice(g * rows, (g + 1) * rows)
            own = jnp.sum(query_ref[c, span].astype(jnp.float32) * fresh_key, axis=1, keepdims=True)
            top_ref[c, span] = jnp.broadcast_to(own, (rows, width))
            mass_ref[c, span] = jnp.ones((rows, width), jnp.float32)
            sum_ref[c, span] = fresh_value

    def attend(step, _):
        pool_copy(step).wait()
        page = iota((rows, step_pages), 1) + step * step_pages
        found = jnp.zeros((rows, step_pages), jnp.float32)
        for m in range(per_row):
            found = found + jnp.where(place_ref[:, m : m + 1] == page, code_ref[:, m : m + 1], 0.0)
        code = jnp.sum(found, axis=0, keepdims=True)
        owner = jnp.floor(code * (1.0 / 32.0))
        live = code - 32.0 * owner
        both = jnp.where(iota((16, step_pages), 0) == 0, owner, live)
        spread = exact_dot(both, spread_ref[...], ((1,), (0,)))
        position = lax.rem(iota((1, tokens), 1), page_size).astype(jnp.float32)
        token_owner = jnp.where(position < spread[1:2], spread[0:1], -1.0)
        row_id = lax.rem(iota((group * rows, 1), 0), rows).astype(jnp.float32)
        chunk = pl.ds(step * step_pages, step_pages)
        for c in range(copies):
            keys = pool_ref[chunk, c, 0].reshape(tokens, width)
            values = pool_ref[chunk, c, 1].reshape(tokens, width)
            scores = lax.dot_general(
                query_ref[c], keys, (((1,), (1,)), ((), ())), preferred_element_type=jnp.float32
            )
            scores = jnp.where(token_owner == row_id, scores, NEVER)
            before = top_ref[c, :, 0:1]
            highest = jnp.maximum(before, jnp.max(scores, axis=1, keepdims=True))
            decay = jnp.exp2((before - highest) * factor)
            weights = jnp.exp2((scores - highest) * factor)
            mass = jnp.sum(weights, axis=1, keepdims=True)
            context = jnp.dot(weights.astype(jnp.bfloat16), values, preferred_element_type=jnp.float32)
            top_ref[c] = jnp.broadcast_to(highest, top_ref.shape[1:])
            mass_ref[c] = mass_ref[c] * decay + mass
            sum_ref[c] = sum_ref[c] * decay + context

        for j in range(3):
            low, high = (tp - 1) * j // 3 + 1, (tp - 1) * (j + 1) // 3 + 1
            pl.when(step == 2 + 2 * j)(lambda low=low, high=high: loop(low, high, stage_one))
            pl.when(step == 4 + 2 * j)(lambda low=low, high=high: loop(low, high, stage_two))
            if j < 2:
                pl.when(step == 6 + 2 * j)(lambda low=low, high=high: loop(low, high, stage_three))
        return 0

    lax.fori_loop(0, steps, attend, 0)

    unpack = jnp.where(
        (iota((padded, extra), 1) == iota((padded, extra), 0) // TILE * moves + lax.rem(iota((padded, extra), 0), TILE))
        & (lax.rem(iota((padded, extra), 0), TILE) < moves),
        1.0, 0.0,
    )
    attended = []
    for h in range(heads):
        c, g = h // group, h % group
        span = slice(g * rows, (g + 1) * rows)
        head = (sum_ref[c, span] / mass_ref[c, span]).astype(jnp.bfloat16)
        answer = exact_dot(unpack, head[slots:], ((1,), (0,)))
        for d in range(ranks):
            reply_ref[d, :, h * width : (h + 1) * width] = answer[d * TILE : (d + 1) * TILE]
        attended.append(head[:slots])

    def reply(k):
        return remote(
            reply_ref.at[peer_rep(k)], replied_ref.at[me], reply_sem.at[0, k], reply_sem.at[1, k], rep=peer_rep(k)
        )

    for k in range(1, ranks):
        reply(k).start()
    replied_ref[pl.ds(me, 1)] = jnp.zeros((1,) + replied_ref.shape[1:], jnp.float32)
    for k in range(1, ranks):
        come = lax.rem(me + ranks - k, ranks)
        remote(replied_ref.at[come], replied_ref.at[come], reply_sem.at[0, k], reply_sem.at[1, k], rep=come).wait_recv()
    home = exact_dot(pick, replied_ref[...].reshape(padded, heads * width), ((0,), (0,)))
    for h in range(heads):
        full = jnp.where(away > 0.0, home[:, h * width : (h + 1) * width], attended[h].astype(jnp.float32))
        gathered_ref[pl.ds(rank, 1), :, h * width : (h + 1) * width] = full.astype(jnp.bfloat16)[None]

    def gather(k):
        return remote(
            gathered_ref.at[rank], gathered_ref.at[rank], gather_sem.at[0, k], gather_sem.at[1, k], tp=peer_tp(k)
        )

    loop(1, tp, lambda k: gather(k).start())
    loop((tp - 1) * 2 // 3 + 1, tp, stage_three)
    loop(1, tp, stage_end)
    own_weight.wait()
    load_residual.wait()

    def gathered(k):
        spot_ref = gathered_ref.at[from_tp(k)]
        remote(spot_ref, spot_ref, gather_sem.at[0, k], gather_sem.at[1, k], tp=from_tp(k)).wait_recv()

    loop(1, tp, gathered)

    strip = next(n for n in (512, 384, 256, 128) if local_width % n == 0)
    square_sum = jnp.zeros((slots, 1), jnp.float32)
    for begin in range(0, local_width, strip):
        span = slice(begin, begin + strip)

        def add(t, total):
            return total + jnp.dot(gathered_ref[t], weight_ref[t, :, span], preferred_element_type=jnp.float32)

        total = residual_ref[:, span].astype(jnp.float32)
        if tp <= 4:
            for t in range(tp):
                total = add(t, total)
        else:
            total = lax.fori_loop(0, tp, add, total)
        total_ref[:, span] = total
        square_sum = square_sum + jnp.sum(total * total, axis=1, keepdims=True)
    square_row = jnp.sum(jnp.where(diagonal, square_sum, 0.0), axis=0, keepdims=True)
    square_ref[...] = jnp.broadcast_to(square_row, square_ref.shape)

    def share(k):
        return remote(square_ref, squares_ref.at[rank], square_sem.at[0, k], square_sem.at[1, k], tp=peer_tp(k))

    loop(1, tp, lambda k: share(k).start())
    squares_ref[pl.ds(rank, 1)] = jnp.broadcast_to(square_row, (1,) + square_ref.shape)

    def shared(k):
        spot_ref = squares_ref.at[from_tp(k)]
        remote(spot_ref, spot_ref, square_sem.at[0, k], square_sem.at[1, k], tp=from_tp(k)).wait_recv()

    loop(1, tp, shared)
    all_row = jnp.sum(squares_ref[...], axis=0)[0:1]
    all_column = jnp.sum(jnp.where(diagonal, all_row, 0.0), axis=1, keepdims=True)
    scale = lax.rsqrt(all_column / (local_width * tp) + EPSILON)
    for begin in range(0, local_width, strip):
        span = slice(begin, begin + strip)
        out_ref[:, span] = (gain_ref[:, span] * (total_ref[:, span] * scale)).astype(out_ref.dtype)

    for k in range(1, ranks):
        ask(k).wait_send()
        reply(k).wait_send()

    def finish(k):
        gather(k).wait_send()
        share(k).wait_send()

    loop(1, tp, finish)


def on_device(
    queries, fresh_kv, kv_pool, page_table, lengths, mig_src, mig_dst, mig_count, residual, out_weight, norm_gain,
):
    tp = lax.axis_size("tp")
    slots, heads, width = queries.shape
    pages, copies, _, page_size, _ = kv_pool.shape
    group = heads // copies
    per_row = page_table.shape[1]
    ranks, capacity = mig_src.shape[1:]
    extra = ranks * capacity // per_row
    rows = slots + extra
    depth, model_width = out_weight.shape
    local_width = model_width // tp
    step_pages = next(n for n in (112, 128, 64, 32, 16) if pages % n == 0)
    tokens = step_pages * page_size
    factor = width ** (-0.5) * math.log2(math.e)

    inputs = jnp.concatenate(
        [queries.reshape(slots, heads * width), fresh_kv.reshape(slots, copies * 2 * width)], axis=1
    )
    small = jnp.stack([
        mig_dst.reshape(-1), mig_src.reshape(-1), jnp.repeat(mig_count[0], capacity), lengths,
    ])
    gain = lax.dynamic_slice_in_dim(norm_gain, lax.axis_index("tp") * local_width, local_width, 0)
    gain = gain.astype(jnp.float32)[None, :]

    vmem = pl.BlockSpec(memory_space=pltpu.VMEM)
    anywhere = pl.BlockSpec(memory_space=pl.ANY)
    scratch = lambda shape, kind: pltpu.VMEM(shape, kind)
    payload = inputs.shape[1] + width
    return pl.pallas_call(
        functools.partial(layer_kernel, ranks, tp, copies, group, step_pages, factor),
        in_specs=[vmem] * 4 + [anywhere] * 3,
        out_specs=vmem,
        out_shape=jax.ShapeDtypeStruct((slots, local_width), jnp.bfloat16),
        scratch_shapes=[
            scratch(kv_pool.shape, jnp.bfloat16),
            scratch((tp, depth, local_width), jnp.bfloat16),
            scratch((slots, local_width), jnp.bfloat16),
            scratch((slots, local_width), jnp.float32),
            scratch((step_pages, tokens), jnp.bfloat16),
            scratch((copies, group * rows, width), jnp.bfloat16),
            scratch((copies, 2, rows, width), jnp.bfloat16),
            scratch((rows, per_row), jnp.int32),
            scratch((rows, per_row), jnp.float32),
            scratch((copies, group * rows, width), jnp.float32),
            scratch((copies, group * rows, width), jnp.float32),
            scratch((copies, group * rows, width), jnp.float32),
            scratch((ranks, TILE, payload), jnp.float32),
            scratch((ranks, TILE, payload), jnp.float32),
            scratch((ranks, TILE, heads * width), jnp.float32),
            scratch((ranks, TILE, heads * width), jnp.float32),
            scratch((tp, slots, heads * width), jnp.bfloat16),
            scratch((TILE, slots), jnp.float32),
            scratch((tp, TILE, slots), jnp.float32),
            pltpu.SemaphoreType.DMA((2,)),
            pltpu.SemaphoreType.DMA((pages // step_pages,)),
            pltpu.SemaphoreType.DMA((2, ranks)),
            pltpu.SemaphoreType.DMA((2, ranks)),
            pltpu.SemaphoreType.DMA((2, tp)),
            pltpu.SemaphoreType.DMA((2, tp)),
            pltpu.SemaphoreType.DMA((9, tp)),
            pltpu.SemaphoreType.DMA((9, tp)),
        ],
        compiler_params=pltpu.CompilerParams(
            collective_id=0, has_side_effects=True, vmem_limit_bytes=56 * 2**20
        ),
    )(inputs, small, page_table, gain, kv_pool, residual, out_weight)


def solution(mesh):
    in_specs = (
        P(("parts", "rep"), "tp", None),
        P(("parts", "rep"), "tp", None, None),
        P(("parts", "rep"), "tp", None, None, None),
        P(("parts", "rep"), None),
        P(("parts", "rep")),
        P(("parts", "rep"), None, None),
        P(("parts", "rep"), None, None),
        P(("parts", "rep"), None),
        P(("parts", "rep"), "tp"),
        P("tp", None),
        P(),
    )
    out_specs = P(("parts", "rep"), "tp")
    return jax.shard_map(
        on_device, mesh=mesh, in_specs=in_specs, out_specs=out_specs, check_vma=False
    )
```

```python
import functools
import math

import jax
import jax.numpy as jnp
from jax import lax
from jax.experimental import pallas as pl
from jax.experimental.pallas import tpu as pltpu
from jax.sharding import PartitionSpec as P

EPSILON = 1e-05
NEVER = -1e30
MESH = pl.DeviceIdType.MESH
TILE = 8


def iota(shape, dimension):
    return lax.broadcasted_iota(jnp.int32, shape, dimension)


def exact_dot(left, right, contract):
    return lax.dot_general(
        left.astype(jnp.bfloat16), right.astype(jnp.bfloat16), (contract, ((), ())), preferred_element_type=jnp.float32
    )


def layer_kernel(
    ranks, tp, copies, group, step_pages, factor,
    flat_query_ref, flat_fresh_ref, flat_table_ref, length_ref, source_ref, target_ref, count_ref, gain_ref,
    pool_hbm, residual_hbm, weight_hbm,
    out_ref, scale_ref,
    pool_ref, weight_ref, residual_ref, gains_ref, spread_ref, inputs_ref, query_ref, table_ref, code_ref,
    top_ref, mass_ref, sum_ref, guest_pages_ref, ask_ref, asked_ref, reply_ref, replied_ref, gathered_ref, square_ref,
    squares_ref,
    local_sem, pool_sem, ask_sem, reply_sem, gather_sem, square_sem, weight_send, weight_recv,
):
    slots, per_row = table_ref.shape
    pages, _, _, page_size, width = pool_hbm.shape
    steps = pages // step_pages
    tokens = step_pages * page_size
    heads = copies * group
    capacity = target_ref.shape[1]
    entries = ranks * capacity
    moves = capacity // per_row
    extra = ranks * moves
    rows = slots
    padded = ranks * TILE
    depth, local_width = weight_ref.shape[1:]
    segment = depth // (2 * ranks)
    half = segment // 2
    third = [((tp - 1) * j // 3 + 1, (tp - 1) * (j + 1) // 3 + 1) for j in range(3)]

    part = lax.axis_index("parts")
    me = lax.axis_index("rep")
    rank = lax.axis_index("tp")
    across_part = 1 - part
    across_rep = lax.rem(me + 2, ranks)
    mate = me + 1 - 2 * lax.rem(me, 2)

    def pool_copy(i):
        spot = pl.ds(i * step_pages, step_pages)
        return pltpu.make_async_copy(pool_hbm.at[spot], pool_ref.at[spot], pool_sem.at[i])

    def peer_rep(k):
        return lax.rem(me + k, ranks)

    def peer_tp(k):
        return lax.rem(rank + k, tp)

    def from_tp(k):
        return lax.rem(rank + tp - k, tp)

    def remote(src, dst, send, recv, **where):
        return pltpu.make_async_remote_copy(
            src_ref=src, dst_ref=dst, send_sem=send, recv_sem=recv, device_id=where, device_id_type=MESH
        )

    barrier = pltpu.get_barrier_semaphore()
    for k in range(1, ranks):
        pl.semaphore_signal(barrier, inc=1, device_id={"rep": peer_rep(k)}, device_id_type=MESH)

    def greet(k, _):
        pl.semaphore_signal(barrier, inc=1, device_id={"tp": peer_tp(k)}, device_id_type=MESH)
        return 0

    lax.fori_loop(1, tp, greet, 0)
    pl.semaphore_signal(barrier, inc=1, device_id={"parts": across_part}, device_id_type=MESH)

    pool_copy(0).start()
    pool_copy(1).start()

    def exact_columns(number, chosen, contract):
        high = jnp.floor(number * (1.0 / 64.0))
        low = number - 64.0 * high
        return 64.0 * exact_dot(high, chosen, contract) + exact_dot(low, chosen, contract)

    diagonal = iota((slots, slots), 0) == iota((slots, slots), 1)
    unit = jnp.where(diagonal, 1.0, 0.0)
    numbers = flat_table_ref[...].astype(jnp.float32)
    high = jnp.floor(numbers * (1.0 / 64.0))
    low = numbers - 64.0 * high
    columns_first = ((1,), (1,))
    table = 64.0 * exact_dot(unit, high, columns_first) + exact_dot(unit, low, columns_first)
    table_ref[...] = table.astype(jnp.int32)
    tile_up = jnp.where(
        iota((capacity, entries), 0) == lax.rem(iota((capacity, entries), 1), capacity), 1.0, 0.0
    )
    tiled = exact_columns(target_ref[...].astype(jnp.float32), tile_up, ((1,), (0,)))
    in_rank = iota((ranks, entries), 1) // capacity == iota((ranks, entries), 0)
    target = jnp.sum(jnp.where(in_rank, tiled, 0.0), axis=0, keepdims=True).astype(jnp.int32)
    count = jnp.zeros((1, entries), jnp.int32)
    for d in range(ranks):
        count = jnp.where(iota((1, entries), 1) // capacity == d, count_ref[:, d : d + 1], count)
    valid = lax.rem(iota((1, entries), 1), capacity) < count
    flat_query = flat_query_ref[...]
    flat_fresh = flat_fresh_ref[...]

    def take(flat, parts, i):
        size = flat.shape[0]
        chosen = jnp.where(iota((slots, size), 1) == iota((slots, size), 0) * parts + i, 1.0, 0.0)
        return exact_dot(chosen, flat, ((1,), (0,))).astype(jnp.bfloat16)

    for h in range(heads):
        rows_of_head = take(flat_query, heads, h)
        inputs_ref[:, h * width : (h + 1) * width] = rows_of_head
        query_ref[h // group, h % group * rows : (h % group + 1) * rows] = rows_of_head
    for i in range(2 * copies):
        inputs_ref[:, (heads + i) * width : (heads + i + 1) * width] = take(flat_fresh, 2 * copies, i)
    listed = jnp.zeros((slots, entries), jnp.float32)
    spot_sum = jnp.zeros((slots, entries), jnp.float32)
    for m in range(per_row):
        same = jnp.where((table_ref[:, m : m + 1] == target) & valid, 1.0, 0.0)
        listed = listed + same
        spot_sum = spot_sum + float(m) * same
    length_row = length_ref[...].astype(jnp.float32)
    length_column = jnp.sum(jnp.where(diagonal, length_row, 0.0), axis=1, keepdims=True)
    spot = jnp.sum(spot_sum, axis=0, keepdims=True)
    entry_length = jnp.sum(listed * length_column, axis=0, keepdims=True)
    filled = jnp.clip(entry_length - page_size * spot, 0.0, float(page_size))
    away = jnp.max(listed, axis=1, keepdims=True)
    row = iota((padded, entries), 0)
    column = iota((padded, entries), 1)
    first = row // TILE * capacity + lax.rem(row, TILE) * per_row
    real = lax.rem(row, TILE) < moves
    head_entry = jnp.where((column == first) & real, 1.0, 0.0)
    pick = exact_dot(head_entry, listed, ((1,), (1,)))
    asking = exact_dot(pick, inputs_ref[...], ((1,), (0,)))
    within = jnp.where((column >= first) & (column < first + per_row) & real, filled, 0.0)
    fold = jnp.where(lax.rem(iota((entries, width), 0), per_row) == iota((entries, width), 1), 1.0, 0.0)
    asking_filled = exact_dot(within, fold, ((1,), (0,)))
    asked_width = inputs_ref.shape[1]
    for d in range(ranks):
        ask_ref[d, :, :asked_width] = asking[d * TILE : (d + 1) * TILE]
        ask_ref[d, :, asked_width:] = asking_filled[d * TILE : (d + 1) * TILE]

    pl.semaphore_wait(barrier, ranks + tp - 1)

    def ask(k):
        return remote(ask_ref.at[peer_rep(k)], asked_ref.at[me], ask_sem.at[0, k], ask_sem.at[1, k], rep=peer_rep(k))

    for k in range(1, ranks):
        ask(k).start()

    mine = part * ranks + me

    def piece(t, owner_part, owner_rep, h):
        begin = pl.multiple_of((owner_part * ranks + owner_rep) * segment + h * half, half)
        return weight_ref.at[t, pl.ds(begin, half)]

    def hop(kind, k, h, spot_ref, **where):
        return remote(spot_ref, spot_ref, weight_send.at[kind, 2 * k + h], weight_recv.at[kind, 2 * k + h], **where)

    def spread_first(k, h):
        other = peer_tp(k)
        begin = pl.multiple_of(mine * segment + h * half, half)
        columns = pl.ds(pl.multiple_of(other * local_width, 128), local_width)
        return remote(
            weight_hbm.at[pl.ds(begin, half), columns], piece(rank, part, me, h),
            weight_send.at[0, 2 * k + h], weight_recv.at[0, 2 * k + h], tp=other,
        )

    def own_first(k, h):
        return hop(1, k, h, piece(from_tp(k), part, me, h), rep=across_rep)

    def own_second(k, h):
        return hop(2, k, h, piece(from_tp(k), part, me, h), parts=across_part)

    def own_mate(k, h):
        return hop(3, k, h, piece(from_tp(k), part, me, h), rep=mate)

    def corner(k, h):
        if h == 0:
            return hop(4, k, h, piece(from_tp(k), part, across_rep, h), parts=across_part)
        return hop(4, k, h, piece(from_tp(k), across_part, me, h), rep=across_rep)

    def first_mate(k, h):
        return hop(5, k, h, piece(from_tp(k), part, across_rep, h), rep=mate)

    def second_mate(k, h):
        return hop(6, k, h, piece(from_tp(k), across_part, me, h), rep=mate)

    def corner_mate(k, h):
        return hop(7, k, h, piece(from_tp(k), across_part, across_rep, h), rep=mate)

    def arrival(kind, k, h, spot_ref):
        hop(kind, k, h, spot_ref, rep=mate).wait_recv()

    def loop(low, high, body):
        def run(k, _):
            body(k)
            return 0

        lax.fori_loop(low, high, run, 0)

    def stage_one(k, h):
        arrival(0, k, h, piece(from_tp(k), part, me, h))
        own_first(k, h).start()
        own_second(k, h).start()
        own_mate(k, h).start()

    def stage_two(k, h):
        arrival(1, k, h, piece(from_tp(k), part, across_rep, h))
        arrival(2, k, h, piece(from_tp(k), across_part, me, h))
        corner(k, h).start()
        first_mate(k, h).start()
        second_mate(k, h).start()

    def stage_three(k, h):
        arrival(4, k, h, piece(from_tp(k), across_part, across_rep, h))
        corner_mate(k, h).start()

    def stage_end(k, h):
        mate_rep = lax.rem(mate + 2, ranks)
        arrival(3, k, h, piece(from_tp(k), part, mate, h))
        arrival(5, k, h, piece(from_tp(k), part, mate_rep, h))
        arrival(6, k, h, piece(from_tp(k), across_part, mate, h))
        arrival(7, k, h, piece(from_tp(k), across_part, mate_rep, h))
        for copy in (
            spread_first, own_first, own_second, own_mate, corner, first_mate, second_mate, corner_mate,
        ):
            copy(k, h).wait_send()

    def stage(body, j):
        loop(*third[j // 2], lambda k: body(k, j % 2))

    stage(lambda k, h: spread_first(k, h).start(), 0)
    stage(lambda k, h: spread_first(k, h).start(), 1)

    for i in range(2, steps):
        pool_copy(i).start()
    gains_ref[...] = gain_ref[...].astype(jnp.float32)
    own_columns = pl.ds(pl.multiple_of(rank * local_width, 128), local_width)
    own_weight = pltpu.make_async_copy(weight_hbm.at[:, own_columns], weight_ref.at[rank], local_sem.at[0])
    own_weight.start()
    load_residual = pltpu.make_async_copy(residual_hbm, residual_ref, local_sem.at[1])
    load_residual.start()

    spread_ref[...] = jnp.where(
        iota((step_pages, tokens), 1) // page_size == iota((step_pages, tokens), 0), 1.0, 0.0
    ).astype(jnp.bfloat16)
    local_filled = jnp.clip(length_column - float(page_size) * iota((slots, per_row), 1).astype(jnp.float32), 0.0, float(page_size))
    local_filled = local_filled * (1.0 - away)
    code_ref[...] = jnp.where(
        local_filled > 0.0, iota((slots, per_row), 0).astype(jnp.float32) * 32.0 + local_filled, 0.0
    )
    for c in range(copies):
        fresh_key = inputs_ref[:, (heads + 2 * c) * width : (heads + 2 * c + 1) * width].astype(jnp.float32)
        fresh_value = inputs_ref[:, (heads + 2 * c + 1) * width : (heads + 2 * c + 2) * width].astype(jnp.float32)
        for g in range(group):
            span = slice(g * rows, (g + 1) * rows)
            own = jnp.sum(query_ref[c, span].astype(jnp.float32) * fresh_key, axis=1, keepdims=True)
            top_ref[c, span] = jnp.broadcast_to(own, (rows, width))
            mass_ref[c, span] = jnp.ones((rows, width), jnp.float32)
            sum_ref[c, span] = fresh_value

    def serve():
        asked_ref[pl.ds(me, 1)] = jnp.zeros((1,) + asked_ref.shape[1:], jnp.float32)
        for k in range(1, ranks):
            come = lax.rem(me + ranks - k, ranks)
            remote(asked_ref.at[come], asked_ref.at[come], ask_sem.at[0, k], ask_sem.at[1, k], rep=come).wait_recv()

        def fetch(i, _):
            for j in range(per_row):
                e = i * per_row + j
                page = jnp.clip(source_ref[e // capacity, lax.rem(e, capacity)], 0, pages - 1)
                guest_pages_ref[pl.ds(e, 1)] = pool_ref[pl.ds(page, 1)]
            return 0

        lax.fori_loop(0, extra, fetch, 0)
        asked = asked_ref[...].reshape(padded, asked_ref.shape[2])
        row = iota((extra, padded), 0)
        pack = jnp.where(iota((extra, padded), 1) == row // moves * TILE + lax.rem(row, moves), 1.0, 0.0)
        guests = exact_dot(pack, asked, ((1,), (0,)))
        held = entries * page_size
        stretch = jnp.where(iota((width, held), 0) == lax.rem(iota((width, held), 1) // page_size, per_row), 1.0, 0.0)
        live = exact_dot(guests[:, asked_width : asked_width + width], stretch, ((1,), (0,)))
        token = iota((extra, held), 1)
        seen = (token // (per_row * page_size) == iota((extra, held), 0)) & (
            lax.rem(token, page_size).astype(jnp.float32) < live
        )
        unpack = jnp.where(
            (iota((padded, extra), 1) == iota((padded, extra), 0) // TILE * moves + lax.rem(iota((padded, extra), 0), TILE))
            & (lax.rem(iota((padded, extra), 0), TILE) < moves),
            1.0, 0.0,
        )
        for c in range(copies):
            fresh_key = guests[:, (heads + 2 * c) * width : (heads + 2 * c + 1) * width]
            fresh_value = guests[:, (heads + 2 * c + 1) * width : (heads + 2 * c + 2) * width]
            keys = guest_pages_ref[:, c, 0].reshape(held, width)
            values = guest_pages_ref[:, c, 1].reshape(held, width)
            for g in range(group):
                h = c * group + g
                query = guests[:, h * width : (h + 1) * width]
                own = jnp.sum(query * fresh_key, axis=1, keepdims=True)
                scores = lax.dot_general(
                    query.astype(jnp.bfloat16), keys, (((1,), (1,)), ((), ())), preferred_element_type=jnp.float32
                )
                scores = jnp.where(seen, scores, NEVER)
                highest = jnp.maximum(own, jnp.max(scores, axis=1, keepdims=True))
                weights = jnp.exp2((scores - highest) * factor)
                own_weight = jnp.exp2((own - highest) * factor)
                mass = own_weight + jnp.sum(weights, axis=1, keepdims=True)
                context = jnp.dot(weights.astype(jnp.bfloat16), values, preferred_element_type=jnp.float32)
                head = (context + own_weight * fresh_value) / mass
                answer = exact_dot(unpack, head, ((1,), (0,)))
                for d in range(ranks):
                    reply_ref[d, :, h * width : (h + 1) * width] = answer[d * TILE : (d + 1) * TILE]
        for k in range(1, ranks):
            reply(k).start()

    def reply(k):
        return remote(
            reply_ref.at[peer_rep(k)], replied_ref.at[me], reply_sem.at[0, k], reply_sem.at[1, k], rep=peer_rep(k)
        )

    middle = steps // 2

    def attend(step, _):
        pl.when(step < middle)(lambda: pool_copy(step).wait())
        page = iota((rows, step_pages), 1) + step * step_pages
        found = jnp.zeros((rows, step_pages), jnp.float32)
        for m in range(per_row):
            found = found + jnp.where(table_ref[:, m : m + 1] == page, code_ref[:, m : m + 1], 0.0)
        code = jnp.sum(found, axis=0, keepdims=True)
        owner = jnp.floor(code * (1.0 / 32.0))
        live = code - 32.0 * owner
        both = jnp.where(iota((16, step_pages), 0) == 0, owner, live)
        spread = exact_dot(both, spread_ref[...], ((1,), (0,)))
        position = lax.rem(iota((1, tokens), 1), page_size).astype(jnp.float32)
        token_owner = jnp.where(position < spread[1:2], spread[0:1], -1.0)
        row_id = lax.rem(iota((group * rows, 1), 0), rows).astype(jnp.float32)
        chunk = pl.ds(step * step_pages, step_pages)
        for c in range(copies):
            keys = pool_ref[chunk, c, 0].reshape(tokens, width)
            values = pool_ref[chunk, c, 1].reshape(tokens, width)
            scores = lax.dot_general(
                query_ref[c], keys, (((1,), (1,)), ((), ())), preferred_element_type=jnp.float32
            )
            scores = jnp.where(token_owner == row_id, scores, NEVER)
            before = top_ref[c, :, 0:1]
            highest = jnp.maximum(before, jnp.max(scores, axis=1, keepdims=True))
            decay = jnp.exp2((before - highest) * factor)
            weights = jnp.exp2((scores - highest) * factor)
            mass = jnp.sum(weights, axis=1, keepdims=True)
            context = jnp.dot(weights.astype(jnp.bfloat16), values, preferred_element_type=jnp.float32)
            top_ref[c] = jnp.broadcast_to(highest, top_ref.shape[1:])
            mass_ref[c] = mass_ref[c] * decay + mass
            sum_ref[c] = sum_ref[c] * decay + context

        for j in range(6):
            if j >= 2:
                pl.when(step == j - 1)(lambda j=j: stage(lambda k, h: spread_first(k, h).start(), j))
            pl.when(step == j + 2)(lambda j=j: stage(stage_one, j))
            if j + 4 < steps:
                pl.when(step == j + 4)(lambda j=j: stage(stage_two, j))
            if j + 6 < steps:
                pl.when(step == j + 6)(lambda j=j: stage(stage_three, j))
        return 0

    def pool_rest():
        for i in range(middle, steps):
            pool_copy(i).wait()
        serve()

    def both_parts(step, _):
        pl.when(step == middle)(pool_rest)
        return attend(step, 0)

    lax.fori_loop(0, steps, both_parts, 0)

    attended = []
    for h in range(heads):
        c, g = h // group, h % group
        span = slice(g * rows, (g + 1) * rows)
        head = (sum_ref[c, span] / mass_ref[c, span]).astype(jnp.bfloat16)
        attended.append(head)

    replied_ref[pl.ds(me, 1)] = jnp.zeros((1,) + replied_ref.shape[1:], jnp.float32)
    for k in range(1, ranks):
        come = lax.rem(me + ranks - k, ranks)
        remote(replied_ref.at[come], replied_ref.at[come], reply_sem.at[0, k], reply_sem.at[1, k], rep=come).wait_recv()
    home = exact_dot(pick, replied_ref[...].reshape(padded, heads * width), ((0,), (0,)))
    for h in range(heads):
        full = jnp.where(away > 0.0, home[:, h * width : (h + 1) * width], attended[h].astype(jnp.float32))
        gathered_ref[pl.ds(rank, 1), :, h * width : (h + 1) * width] = full.astype(jnp.bfloat16)[None]

    def gather(k):
        return remote(
            gathered_ref.at[rank], gathered_ref.at[rank], gather_sem.at[0, k], gather_sem.at[1, k], tp=peer_tp(k)
        )

    loop(1, tp, lambda k: gather(k).start())
    for j in range(6):
        if j + 4 >= steps:
            stage(stage_two, j)
    for j in range(6):
        if j + 6 >= steps:
            stage(stage_three, j)
    for j in range(6):
        stage(stage_end, j)
    own_weight.wait()
    load_residual.wait()

    def gathered(k):
        spot_ref = gathered_ref.at[from_tp(k)]
        remote(spot_ref, spot_ref, gather_sem.at[0, k], gather_sem.at[1, k], tp=from_tp(k)).wait_recv()

    loop(1, tp, gathered)

    strip = next(n for n in (512, 384, 256, 128) if local_width % n == 0)
    square_sum = jnp.zeros((slots, 1), jnp.float32)
    for begin in range(0, local_width, strip):
        span = slice(begin, begin + strip)

        def add(t, total):
            return total + jnp.dot(gathered_ref[t], weight_ref[t, :, span], preferred_element_type=jnp.float32)

        total = residual_ref[:, span].astype(jnp.float32)
        if tp <= 4:
            for t in range(tp):
                total = add(t, total)
        else:
            total = lax.fori_loop(0, tp, add, total)
        for j in range(0, strip, 128):
            tile = slice(begin + j, begin + j + 128)
            gain = gains_ref[pl.ds((rank * local_width + begin + j) // 128, 1), :]
            out_ref[:, tile] = total[:, j : j + 128] * gain
        square_sum = square_sum + jnp.sum(total * total, axis=1, keepdims=True)
    square_row = jnp.sum(jnp.where(diagonal, square_sum, 0.0), axis=0, keepdims=True)
    square_ref[...] = jnp.broadcast_to(square_row, square_ref.shape)

    def share(k):
        return remote(square_ref, squares_ref.at[rank], square_sem.at[0, k], square_sem.at[1, k], tp=peer_tp(k))

    loop(1, tp, lambda k: share(k).start())
    squares_ref[pl.ds(rank, 1)] = jnp.broadcast_to(square_row, (1,) + square_ref.shape)

    def shared(k):
        spot_ref = squares_ref.at[from_tp(k)]
        remote(spot_ref, spot_ref, square_sem.at[0, k], square_sem.at[1, k], tp=from_tp(k)).wait_recv()

    loop(1, tp, shared)
    all_row = jnp.sum(squares_ref[...], axis=0)[0:1]
    all_column = jnp.sum(jnp.where(diagonal, all_row, 0.0), axis=1, keepdims=True)
    scale_ref[...] = lax.rsqrt(all_column / (local_width * tp) + EPSILON)
    for k in range(1, ranks):
        ask(k).wait_send()
        reply(k).wait_send()

    def finish(k):
        gather(k).wait_send()
        share(k).wait_send()

    loop(1, tp, finish)


def on_device(
    queries, fresh_kv, kv_pool, page_table, lengths, mig_src, mig_dst, mig_count, residual, out_weight, norm_gain,
):
    tp = lax.axis_size("tp")
    slots, heads, width = queries.shape
    pages, copies, _, page_size, _ = kv_pool.shape
    group = heads // copies
    per_row = page_table.shape[1]
    ranks, capacity = mig_src.shape[1:]
    depth, model_width = out_weight.shape
    local_width = model_width // tp
    step_pages = next(n for n in (112, 128, 64, 32, 16) if pages % n == 0)
    tokens = step_pages * page_size
    factor = width ** (-0.5) * math.log2(math.e)

    vmem = pl.BlockSpec(memory_space=pltpu.VMEM)
    anywhere = pl.BlockSpec(memory_space=pl.ANY)
    scratch = lambda shape, kind: pltpu.VMEM(shape, kind)
    asked_width = (heads + 2 * copies) * width
    payload = asked_width + width
    total, scale = pl.pallas_call(
        functools.partial(layer_kernel, ranks, tp, copies, group, step_pages, factor),
        in_specs=[vmem] * 4 + [pl.BlockSpec(memory_space=pltpu.SMEM)] + [vmem] * 3 + [anywhere] * 3,
        out_specs=[vmem] * 2,
        out_shape=[
            jax.ShapeDtypeStruct((slots, local_width), jnp.float32), jax.ShapeDtypeStruct((slots, 1), jnp.float32),
        ],
        scratch_shapes=[
            scratch(kv_pool.shape, jnp.bfloat16),
            scratch((tp, depth, local_width), jnp.bfloat16),
            scratch((slots, local_width), jnp.bfloat16),
            scratch((model_width // 128, 128), jnp.float32),
            scratch((step_pages, tokens), jnp.bfloat16),
            scratch((slots, asked_width), jnp.bfloat16),
            scratch((copies, heads // copies * slots, width), jnp.bfloat16),
            scratch((slots, per_row), jnp.int32),
            scratch((slots, per_row), jnp.float32),
            scratch((copies, group * slots, width), jnp.float32),
            scratch((copies, group * slots, width), jnp.float32),
            scratch((copies, group * slots, width), jnp.float32),
            scratch((ranks * capacity,) + kv_pool.shape[1:], jnp.bfloat16),
            scratch((ranks, TILE, payload), jnp.float32),
            scratch((ranks, TILE, payload), jnp.float32),
            scratch((ranks, TILE, heads * width), jnp.float32),
            scratch((ranks, TILE, heads * width), jnp.float32),
            scratch((tp, slots, heads * width), jnp.bfloat16),
            scratch((TILE, slots), jnp.float32),
            scratch((tp, TILE, slots), jnp.float32),
            pltpu.SemaphoreType.DMA((2,)),
            pltpu.SemaphoreType.DMA((pages // step_pages,)),
            pltpu.SemaphoreType.DMA((2, ranks)),
            pltpu.SemaphoreType.DMA((2, ranks)),
            pltpu.SemaphoreType.DMA((2, tp)),
            pltpu.SemaphoreType.DMA((2, tp)),
            pltpu.SemaphoreType.DMA((8, 2 * tp)),
            pltpu.SemaphoreType.DMA((8, 2 * tp)),
        ],
        compiler_params=pltpu.CompilerParams(
            collective_id=0, has_side_effects=True, vmem_limit_bytes=56 * 2**20
        ),
    )(
        queries.reshape(-1, width), fresh_kv.reshape(-1, width), page_table.T, lengths[None, :], mig_src[0], mig_dst[0],
        mig_count, norm_gain.reshape(-1, 128), kv_pool, residual, out_weight,
    )
    return (total * scale).astype(jnp.bfloat16)


def solution(mesh):
    in_specs = (
        P(("parts", "rep"), "tp", None),
        P(("parts", "rep"), "tp", None, None),
        P(("parts", "rep"), "tp", None, None, None),
        P(("parts", "rep"), None),
        P(("parts", "rep")),
        P(("parts", "rep"), None, None),
        P(("parts", "rep"), None, None),
        P(("parts", "rep"), None),
        P(("parts", "rep"), "tp"),
        P("tp", None),
        P(),
    )
    out_specs = P(("parts", "rep"), "tp")
    return jax.shard_map(
        on_device, mesh=mesh, in_specs=in_specs, out_specs=out_specs, check_vma=False
    )
```

```python
import functools
import math

import jax
import jax.numpy as jnp
from jax import lax
from jax.experimental import pallas as pl
from jax.experimental.pallas import tpu as pltpu
from jax.sharding import PartitionSpec as P

EPSILON = 1e-05
NEVER = -1e30
MESH = pl.DeviceIdType.MESH
TILE = 8


def iota(shape, dimension):
    return lax.broadcasted_iota(jnp.int32, shape, dimension)


def exact_dot(left, right, contract):
    return lax.dot_general(
        left.astype(jnp.bfloat16), right.astype(jnp.bfloat16), (contract, ((), ())), preferred_element_type=jnp.float32
    )


def layer_kernel(
    ranks, tp, copies, group, step_pages, factor,
    flat_query_ref, flat_fresh_ref, flat_table_ref, length_ref, source_ref, target_ref, count_ref, gain_ref,
    pool_hbm, residual_hbm, weight_hbm,
    result_ref,
    out_ref, pool_ref, weight_ref, residual_ref, gains_ref, spread_ref, inputs_ref, query_ref, table_ref, code_ref,
    top_ref, mass_ref, sum_ref, guest_pages_ref, ask_ref, asked_ref, reply_ref, replied_ref, gathered_ref, square_ref,
    squares_ref,
    local_sem, pool_sem, ask_sem, reply_sem, gather_sem, square_sem, weight_send, weight_recv,
):
    slots, per_row = table_ref.shape
    pages, _, _, page_size, width = pool_hbm.shape
    steps = pages // step_pages
    tokens = step_pages * page_size
    heads = copies * group
    capacity = target_ref.shape[1]
    entries = ranks * capacity
    moves = capacity // per_row
    extra = ranks * moves
    rows = slots
    padded = ranks * TILE
    depth, local_width = weight_ref.shape[1:]
    segment = depth // (2 * ranks)
    half = segment // 2
    third = [((tp - 1) * j // 3 + 1, (tp - 1) * (j + 1) // 3 + 1) for j in (0, 2, 1)]

    part = lax.axis_index("parts")
    me = lax.axis_index("rep")
    rank = lax.axis_index("tp")
    across_part = 1 - part
    across_rep = lax.rem(me + 2, ranks)
    mate = me + 1 - 2 * lax.rem(me, 2)

    def pool_copy(i):
        spot = pl.ds(i * step_pages, step_pages)
        return pltpu.make_async_copy(pool_hbm.at[spot], pool_ref.at[spot], pool_sem.at[i])

    def peer_rep(k):
        return lax.rem(me + k, ranks)

    def peer_tp(k):
        return lax.rem(rank + k, tp)

    def from_tp(k):
        return lax.rem(rank + tp - k, tp)

    def remote(src, dst, send, recv, **where):
        return pltpu.make_async_remote_copy(
            src_ref=src, dst_ref=dst, send_sem=send, recv_sem=recv, device_id=where, device_id_type=MESH
        )

    barrier = pltpu.get_barrier_semaphore()
    for k in range(1, ranks):
        pl.semaphore_signal(barrier, inc=1, device_id={"rep": peer_rep(k)}, device_id_type=MESH)

    def greet(k, _):
        pl.semaphore_signal(barrier, inc=1, device_id={"tp": peer_tp(k)}, device_id_type=MESH)
        return 0

    lax.fori_loop(1, tp, greet, 0)
    pl.semaphore_signal(barrier, inc=1, device_id={"parts": across_part}, device_id_type=MESH)

    pool_copy(0).start()
    pool_copy(1).start()
    pl.semaphore_wait(barrier, ranks + tp - 1)

    mine = part * ranks + me

    def piece(t, owner_part, owner_rep, h):
        begin = pl.multiple_of((owner_part * ranks + owner_rep) * segment + h * half, half)
        return weight_ref.at[t, pl.ds(begin, half)]

    def hop(kind, k, h, spot_ref, **where):
        return remote(spot_ref, spot_ref, weight_send.at[kind, 2 * k + h], weight_recv.at[kind, 2 * k + h], **where)

    def spread_first(k, h):
        other = peer_tp(k)
        begin = pl.multiple_of(mine * segment + h * half, half)
        columns = pl.ds(pl.multiple_of(other * local_width, 128), local_width)
        return remote(
            weight_hbm.at[pl.ds(begin, half), columns], piece(rank, part, me, h),
            weight_send.at[0, 2 * k + h], weight_recv.at[0, 2 * k + h], tp=other,
        )

    def own_first(k, h):
        return hop(1, k, h, piece(from_tp(k), part, me, h), rep=across_rep)

    def own_second(k, h):
        return hop(2, k, h, piece(from_tp(k), part, me, h), parts=across_part)

    def own_mate(k, h):
        return hop(3, k, h, piece(from_tp(k), part, me, h), rep=mate)

    def corner(k, h):
        if h == 0:
            return hop(4, k, h, piece(from_tp(k), part, across_rep, h), parts=across_part)
        return hop(4, k, h, piece(from_tp(k), across_part, me, h), rep=across_rep)

    def first_mate(k, h):
        return hop(5, k, h, piece(from_tp(k), part, across_rep, h), rep=mate)

    def second_mate(k, h):
        return hop(6, k, h, piece(from_tp(k), across_part, me, h), rep=mate)

    def corner_mate(k, h):
        return hop(7, k, h, piece(from_tp(k), across_part, across_rep, h), rep=mate)

    def arrival(kind, k, h, spot_ref):
        hop(kind, k, h, spot_ref, rep=mate).wait_recv()

    def loop(low, high, body):
        def run(k, _):
            body(k)
            return 0

        lax.fori_loop(low, high, run, 0)

    def stage_one(k, h):
        arrival(0, k, h, piece(from_tp(k), part, me, h))
        own_first(k, h).start()
        own_second(k, h).start()
        own_mate(k, h).start()

    def spread_start(k, h):
        spread_first(k, h).start()

    def stage_two(k, h):
        arrival(1, k, h, piece(from_tp(k), part, across_rep, h))
        arrival(2, k, h, piece(from_tp(k), across_part, me, h))
        corner(k, h).start()
        first_mate(k, h).start()
        second_mate(k, h).start()

    def stage_three(k, h):
        arrival(4, k, h, piece(from_tp(k), across_part, across_rep, h))
        corner_mate(k, h).start()

    def stage_end(k, h):
        mate_rep = lax.rem(mate + 2, ranks)
        arrival(3, k, h, piece(from_tp(k), part, mate, h))
        arrival(5, k, h, piece(from_tp(k), part, mate_rep, h))
        arrival(6, k, h, piece(from_tp(k), across_part, mate, h))
        arrival(7, k, h, piece(from_tp(k), across_part, mate_rep, h))
        for copy in (
            spread_first, own_first, own_second, own_mate, corner, first_mate, second_mate, corner_mate,
        ):
            copy(k, h).wait_send()

    def stage(body, j):
        loop(*third[j // 2], lambda k: body(k, j % 2))

    stage(spread_start, 0)
    stage(spread_start, 1)

    stage(spread_start, 2)
    for i in range(2, steps):
        pool_copy(i).start()

    def exact_columns(number, chosen, contract):
        high = jnp.floor(number * (1.0 / 64.0))
        low = number - 64.0 * high
        return 64.0 * exact_dot(high, chosen, contract) + exact_dot(low, chosen, contract)

    diagonal = iota((slots, slots), 0) == iota((slots, slots), 1)
    unit = jnp.where(diagonal, 1.0, 0.0)
    numbers = flat_table_ref[...].astype(jnp.float32)
    high = jnp.floor(numbers * (1.0 / 64.0))
    low = numbers - 64.0 * high
    columns_first = ((1,), (1,))
    table = 64.0 * exact_dot(unit, high, columns_first) + exact_dot(unit, low, columns_first)
    table_ref[...] = table.astype(jnp.int32)
    tile_up = jnp.where(
        iota((capacity, entries), 0) == lax.rem(iota((capacity, entries), 1), capacity), 1.0, 0.0
    )
    tiled = exact_columns(target_ref[...].astype(jnp.float32), tile_up, ((1,), (0,)))
    in_rank = iota((ranks, entries), 1) // capacity == iota((ranks, entries), 0)
    target = jnp.sum(jnp.where(in_rank, tiled, 0.0), axis=0, keepdims=True).astype(jnp.int32)
    count = jnp.zeros((1, entries), jnp.int32)
    for d in range(ranks):
        count = jnp.where(iota((1, entries), 1) // capacity == d, count_ref[:, d : d + 1], count)
    valid = lax.rem(iota((1, entries), 1), capacity) < count
    flat_query = flat_query_ref[...]
    flat_fresh = flat_fresh_ref[...]

    def take(flat, parts, i):
        size = flat.shape[0]
        chosen = jnp.where(iota((slots, size), 1) == iota((slots, size), 0) * parts + i, 1.0, 0.0)
        return exact_dot(chosen, flat, ((1,), (0,))).astype(jnp.bfloat16)

    for h in range(heads):
        rows_of_head = take(flat_query, heads, h)
        inputs_ref[:, h * width : (h + 1) * width] = rows_of_head
        query_ref[h // group, h % group * rows : (h % group + 1) * rows] = rows_of_head
    for i in range(2 * copies):
        inputs_ref[:, (heads + i) * width : (heads + i + 1) * width] = take(flat_fresh, 2 * copies, i)
    listed = jnp.zeros((slots, entries), jnp.float32)
    spot_sum = jnp.zeros((slots, entries), jnp.float32)
    for m in range(per_row):
        same = jnp.where((table_ref[:, m : m + 1] == target) & valid, 1.0, 0.0)
        listed = listed + same
        spot_sum = spot_sum + float(m) * same
    length_row = length_ref[...].astype(jnp.float32)
    length_column = jnp.sum(jnp.where(diagonal, length_row, 0.0), axis=1, keepdims=True)
    spot = jnp.sum(spot_sum, axis=0, keepdims=True)
    entry_length = jnp.sum(listed * length_column, axis=0, keepdims=True)
    filled = jnp.clip(entry_length - page_size * spot, 0.0, float(page_size))
    away = jnp.max(listed, axis=1, keepdims=True)
    row = iota((padded, entries), 0)
    column = iota((padded, entries), 1)
    first = row // TILE * capacity + lax.rem(row, TILE) * per_row
    real = lax.rem(row, TILE) < moves
    head_entry = jnp.where((column == first) & real, 1.0, 0.0)
    pick = exact_dot(head_entry, listed, ((1,), (1,)))
    asking = exact_dot(pick, inputs_ref[...], ((1,), (0,)))
    within = jnp.where((column >= first) & (column < first + per_row) & real, filled, 0.0)
    fold = jnp.where(lax.rem(iota((entries, width), 0), per_row) == iota((entries, width), 1), 1.0, 0.0)
    asking_filled = exact_dot(within, fold, ((1,), (0,)))
    asked_width = inputs_ref.shape[1]
    for d in range(ranks):
        ask_ref[d, :, :asked_width] = asking[d * TILE : (d + 1) * TILE]
        ask_ref[d, :, asked_width:] = asking_filled[d * TILE : (d + 1) * TILE]

    def ask(k):
        return remote(ask_ref.at[peer_rep(k)], asked_ref.at[me], ask_sem.at[0, k], ask_sem.at[1, k], rep=peer_rep(k))

    for k in range(1, ranks):
        ask(k).start()
    stage(stage_one, 0)
    stage(spread_start, 3)

    gains_ref[...] = gain_ref[...].astype(jnp.float32)
    own_columns = pl.ds(pl.multiple_of(rank * local_width, 128), local_width)
    own_weight = pltpu.make_async_copy(weight_hbm.at[:, own_columns], weight_ref.at[rank], local_sem.at[0])
    own_weight.start()
    load_residual = pltpu.make_async_copy(residual_hbm, residual_ref, local_sem.at[1])
    load_residual.start()

    spread_ref[...] = jnp.where(
        iota((step_pages, tokens), 1) // page_size == iota((step_pages, tokens), 0), 1.0, 0.0
    ).astype(jnp.bfloat16)
    local_filled = jnp.clip(length_column - float(page_size) * iota((slots, per_row), 1).astype(jnp.float32), 0.0, float(page_size))
    local_filled = local_filled * (1.0 - away)
    code_ref[...] = jnp.where(
        local_filled > 0.0, iota((slots, per_row), 0).astype(jnp.float32) * 32.0 + local_filled, 0.0
    )
    for c in range(copies):
        fresh_key = inputs_ref[:, (heads + 2 * c) * width : (heads + 2 * c + 1) * width].astype(jnp.float32)
        fresh_value = inputs_ref[:, (heads + 2 * c + 1) * width : (heads + 2 * c + 2) * width].astype(jnp.float32)
        for g in range(group):
            span = slice(g * rows, (g + 1) * rows)
            own = jnp.sum(query_ref[c, span].astype(jnp.float32) * fresh_key, axis=1, keepdims=True)
            top_ref[c, span] = jnp.broadcast_to(own, (rows, width))
            mass_ref[c, span] = jnp.ones((rows, width), jnp.float32)
            sum_ref[c, span] = fresh_value

    def serve():
        asked_ref[pl.ds(me, 1)] = jnp.zeros((1,) + asked_ref.shape[1:], jnp.float32)
        for k in range(1, ranks):
            come = lax.rem(me + ranks - k, ranks)
            remote(asked_ref.at[come], asked_ref.at[come], ask_sem.at[0, k], ask_sem.at[1, k], rep=come).wait_recv()

        def fetch(i, _):
            for j in range(per_row):
                e = i * per_row + j
                page = jnp.clip(source_ref[e // capacity, lax.rem(e, capacity)], 0, pages - 1)
                guest_pages_ref[pl.ds(e, 1)] = pool_ref[pl.ds(page, 1)]
            return 0

        lax.fori_loop(0, extra, fetch, 0)
        asked = asked_ref[...].reshape(padded, asked_ref.shape[2])
        row = iota((extra, padded), 0)
        pack = jnp.where(iota((extra, padded), 1) == row // moves * TILE + lax.rem(row, moves), 1.0, 0.0)
        guests = exact_dot(pack, asked, ((1,), (0,)))
        held = entries * page_size
        stretch = jnp.where(iota((width, held), 0) == lax.rem(iota((width, held), 1) // page_size, per_row), 1.0, 0.0)
        live = exact_dot(guests[:, asked_width : asked_width + width], stretch, ((1,), (0,)))
        token = iota((extra, held), 1)
        seen = (token // (per_row * page_size) == iota((extra, held), 0)) & (
            lax.rem(token, page_size).astype(jnp.float32) < live
        )
        unpack = jnp.where(
            (iota((padded, extra), 1) == iota((padded, extra), 0) // TILE * moves + lax.rem(iota((padded, extra), 0), TILE))
            & (lax.rem(iota((padded, extra), 0), TILE) < moves),
            1.0, 0.0,
        )
        for c in range(copies):
            fresh_key = guests[:, (heads + 2 * c) * width : (heads + 2 * c + 1) * width]
            fresh_value = guests[:, (heads + 2 * c + 1) * width : (heads + 2 * c + 2) * width]
            keys = guest_pages_ref[:, c, 0].reshape(held, width)
            values = guest_pages_ref[:, c, 1].reshape(held, width)
            for g in range(group):
                h = c * group + g
                query = guests[:, h * width : (h + 1) * width]
                own = jnp.sum(query * fresh_key, axis=1, keepdims=True)
                scores = lax.dot_general(
                    query.astype(jnp.bfloat16), keys, (((1,), (1,)), ((), ())), preferred_element_type=jnp.float32
                )
                scores = jnp.where(seen, scores, NEVER)
                highest = jnp.maximum(own, jnp.max(scores, axis=1, keepdims=True))
                weights = jnp.exp2((scores - highest) * factor)
                own_weight = jnp.exp2((own - highest) * factor)
                mass = own_weight + jnp.sum(weights, axis=1, keepdims=True)
                context = jnp.dot(weights.astype(jnp.bfloat16), values, preferred_element_type=jnp.float32)
                head = (context + own_weight * fresh_value) / mass
                answer = exact_dot(unpack, head, ((1,), (0,)))
                for d in range(ranks):
                    reply_ref[d, :, h * width : (h + 1) * width] = answer[d * TILE : (d + 1) * TILE]
        for k in range(1, ranks):
            reply(k).start()

    def reply(k):
        return remote(
            reply_ref.at[peer_rep(k)], replied_ref.at[me], reply_sem.at[0, k], reply_sem.at[1, k], rep=peer_rep(k)
        )

    stage(stage_one, 1)
    stage(spread_start, 4)
    middle = steps // 2

    def attend(step, _):
        pl.when(step < middle)(lambda: pool_copy(step).wait())
        page = iota((rows, step_pages), 1) + step * step_pages
        found = jnp.zeros((rows, step_pages), jnp.float32)
        for m in range(per_row):
            found = found + jnp.where(table_ref[:, m : m + 1] == page, code_ref[:, m : m + 1], 0.0)
        code = jnp.sum(found, axis=0, keepdims=True)
        owner = jnp.floor(code * (1.0 / 32.0))
        live = code - 32.0 * owner
        both = jnp.where(iota((16, step_pages), 0) == 0, owner, live)
        spread = exact_dot(both, spread_ref[...], ((1,), (0,)))
        position = lax.rem(iota((1, tokens), 1), page_size).astype(jnp.float32)
        token_owner = jnp.where(position < spread[1:2], spread[0:1], -1.0)
        row_id = lax.rem(iota((group * rows, 1), 0), rows).astype(jnp.float32)
        chunk = pl.ds(step * step_pages, step_pages)
        ones = jnp.ones((tokens, width), jnp.bfloat16)
        all_scores = []
        for c in range(copies):
            keys = pool_ref[chunk, c, 0].reshape(tokens, width)
            all_scores.append(lax.dot_general(
                query_ref[c], keys, (((1,), (1,)), ((), ())), preferred_element_type=jnp.float32
            ))
        for c in range(copies):
            values = pool_ref[chunk, c, 1].reshape(tokens, width)
            scores = jnp.where(token_owner == row_id, all_scores[c], NEVER)
            before = top_ref[c]
            highest = jnp.maximum(before, jnp.max(scores, axis=1, keepdims=True))
            decay = jnp.exp2((before - highest) * factor)
            weights = jnp.exp2((scores - highest[:, 0:1]) * factor).astype(jnp.bfloat16)
            both = jnp.dot(weights, jnp.concatenate([values, ones], axis=1), preferred_element_type=jnp.float32)
            top_ref[c] = highest
            mass_ref[c] = mass_ref[c] * decay + both[:, width:]
            sum_ref[c] = sum_ref[c] * decay + both[:, :width]

        def at(when, body, j):
            pl.when(step == when)(lambda: stage(body, j))

        for when, body, j in (
            (0, stage_one, 2), (0, spread_start, 5), (1, stage_two, 0), (2, stage_two, 1), (3, stage_one, 3),
            (4, stage_three, 0), (5, stage_two, 2), (6, stage_one, 4), (7, stage_three, 1), (7, stage_two, 3),
            (9, stage_one, 5), (9, stage_three, 2),
        ):
            at(when, body, j)
        return 0

    def pool_rest():
        for i in range(middle, steps):
            pool_copy(i).wait()
        serve()

    def both_parts(step, _):
        pl.when(step == middle)(pool_rest)
        return attend(step, 0)

    lax.fori_loop(0, steps, both_parts, 0)

    attended = []
    for h in range(heads):
        c, g = h // group, h % group
        span = slice(g * rows, (g + 1) * rows)
        head = (sum_ref[c, span] / mass_ref[c, span]).astype(jnp.bfloat16)
        attended.append(head)

    replied_ref[pl.ds(me, 1)] = jnp.zeros((1,) + replied_ref.shape[1:], jnp.float32)
    for k in range(1, ranks):
        come = lax.rem(me + ranks - k, ranks)
        remote(replied_ref.at[come], replied_ref.at[come], reply_sem.at[0, k], reply_sem.at[1, k], rep=come).wait_recv()
    home = exact_dot(pick, replied_ref[...].reshape(padded, heads * width), ((0,), (0,)))
    for h in range(heads):
        full = jnp.where(away > 0.0, home[:, h * width : (h + 1) * width], attended[h].astype(jnp.float32))
        gathered_ref[pl.ds(rank, 1), :, h * width : (h + 1) * width] = full.astype(jnp.bfloat16)[None]

    def gather(k):
        return remote(
            gathered_ref.at[rank], gathered_ref.at[rank], gather_sem.at[0, k], gather_sem.at[1, k], tp=peer_tp(k)
        )

    loop(1, tp, lambda k: gather(k).start())
    stage(stage_two, 4)
    stage(stage_three, 3)
    own_weight.wait()
    load_residual.wait()
    strip = next(n for n in (512, 384, 256, 128) if local_width % n == 0)
    spans = [slice(begin, begin + strip) for begin in range(0, local_width, strip)]

    def product(t, span):
        return jnp.dot(gathered_ref[t], weight_ref[t, :, span], preferred_element_type=jnp.float32)

    def products(j, span):
        low, high = third[j]
        total = out_ref[:, span]
        if high - low == 1:
            return total + product(from_tp(low), span)
        return lax.fori_loop(low, high, lambda k, total: total + product(from_tp(k), span), total)

    def gathered(k):
        spot_ref = gathered_ref.at[from_tp(k)]
        remote(spot_ref, spot_ref, gather_sem.at[0, k], gather_sem.at[1, k], tp=from_tp(k)).wait_recv()

    for span in spans:
        out_ref[:, span] = residual_ref[:, span].astype(jnp.float32) + product(rank, span)
    stage(stage_two, 5)
    stage(stage_three, 4)
    loop(1, tp, gathered)
    stage(stage_end, 0)
    stage(stage_end, 1)
    for span in spans:
        out_ref[:, span] = products(0, span)
    stage(stage_three, 5)
    stage(stage_end, 2)
    stage(stage_end, 3)
    for span in spans:
        out_ref[:, span] = products(1, span)
    stage(stage_end, 4)
    stage(stage_end, 5)
    square_sum = jnp.zeros((slots, 1), jnp.float32)
    for span in spans:
        total = products(2, span)
        square_sum = square_sum + jnp.sum(total * total, axis=1, keepdims=True)
        for j in range(0, strip, 128):
            tile = slice(span.start + j, span.start + j + 128)
            gain = gains_ref[pl.ds((rank * local_width + span.start + j) // 128, 1), :]
            out_ref[:, tile] = total[:, j : j + 128] * gain
    square_row = jnp.sum(jnp.where(diagonal, square_sum, 0.0), axis=0, keepdims=True)
    square_ref[...] = jnp.broadcast_to(square_row, square_ref.shape)

    def share(k):
        return remote(square_ref, squares_ref.at[rank], square_sem.at[0, k], square_sem.at[1, k], tp=peer_tp(k))

    loop(1, tp, lambda k: share(k).start())
    squares_ref[pl.ds(rank, 1)] = jnp.broadcast_to(square_row, (1,) + square_ref.shape)

    def shared(k):
        spot_ref = squares_ref.at[from_tp(k)]
        remote(spot_ref, spot_ref, square_sem.at[0, k], square_sem.at[1, k], tp=from_tp(k)).wait_recv()

    loop(1, tp, shared)
    all_row = jnp.sum(squares_ref[...], axis=0)[0:1]
    all_column = jnp.sum(jnp.where(diagonal, all_row, 0.0), axis=1, keepdims=True)
    scale = lax.rsqrt(all_column / (local_width * tp) + EPSILON)
    for span in spans:
        result_ref[:, span] = (out_ref[:, span] * scale).astype(result_ref.dtype)
    for k in range(1, ranks):
        ask(k).wait_send()
        reply(k).wait_send()

    def finish(k):
        gather(k).wait_send()
        share(k).wait_send()

    loop(1, tp, finish)


def on_device(
    queries, fresh_kv, kv_pool, page_table, lengths, mig_src, mig_dst, mig_count, residual, out_weight, norm_gain,
):
    tp = lax.axis_size("tp")
    slots, heads, width = queries.shape
    pages, copies, _, page_size, _ = kv_pool.shape
    group = heads // copies
    per_row = page_table.shape[1]
    ranks, capacity = mig_src.shape[1:]
    depth, model_width = out_weight.shape
    local_width = model_width // tp
    step_pages = next(n for n in (112, 128, 64, 32, 16) if pages % n == 0)
    tokens = step_pages * page_size
    factor = width ** (-0.5) * math.log2(math.e)

    vmem = pl.BlockSpec(memory_space=pltpu.VMEM)
    anywhere = pl.BlockSpec(memory_space=pl.ANY)
    scratch = lambda shape, kind: pltpu.VMEM(shape, kind)
    asked_width = (heads + 2 * copies) * width
    payload = asked_width + width
    return pl.pallas_call(
        functools.partial(layer_kernel, ranks, tp, copies, group, step_pages, factor),
        in_specs=[vmem] * 4 + [pl.BlockSpec(memory_space=pltpu.SMEM)] + [vmem] * 3 + [anywhere] * 3,
        out_specs=vmem,
        out_shape=jax.ShapeDtypeStruct((slots, local_width), jnp.bfloat16),
        scratch_shapes=[
            scratch((slots, local_width), jnp.float32),
            scratch(kv_pool.shape, jnp.bfloat16),
            scratch((tp, depth, local_width), jnp.bfloat16),
            scratch((slots, local_width), jnp.bfloat16),
            scratch((model_width // 128, 128), jnp.float32),
            scratch((step_pages, tokens), jnp.bfloat16),
            scratch((slots, asked_width), jnp.bfloat16),
            scratch((copies, heads // copies * slots, width), jnp.bfloat16),
            scratch((slots, per_row), jnp.int32),
            scratch((slots, per_row), jnp.float32),
            scratch((copies, group * slots, width), jnp.float32),
            scratch((copies, group * slots, width), jnp.float32),
            scratch((copies, group * slots, width), jnp.float32),
            scratch((ranks * capacity,) + kv_pool.shape[1:], jnp.bfloat16),
            scratch((ranks, TILE, payload), jnp.float32),
            scratch((ranks, TILE, payload), jnp.float32),
            scratch((ranks, TILE, heads * width), jnp.float32),
            scratch((ranks, TILE, heads * width), jnp.float32),
            scratch((tp, slots, heads * width), jnp.bfloat16),
            scratch((TILE, slots), jnp.float32),
            scratch((tp, TILE, slots), jnp.float32),
            pltpu.SemaphoreType.DMA((2,)),
            pltpu.SemaphoreType.DMA((pages // step_pages,)),
            pltpu.SemaphoreType.DMA((2, ranks)),
            pltpu.SemaphoreType.DMA((2, ranks)),
            pltpu.SemaphoreType.DMA((2, tp)),
            pltpu.SemaphoreType.DMA((2, tp)),
            pltpu.SemaphoreType.DMA((8, 2 * tp)),
            pltpu.SemaphoreType.DMA((8, 2 * tp)),
        ],
        compiler_params=pltpu.CompilerParams(
            collective_id=0, has_side_effects=True, vmem_limit_bytes=56 * 2**20
        ),
    )(
        queries.reshape(-1, width), fresh_kv.reshape(-1, width), page_table.T, lengths[None, :], mig_src[0], mig_dst[0],
        mig_count, norm_gain.reshape(-1, 128), kv_pool, residual, out_weight,
    )


def solution(mesh):
    in_specs = (
        P(("parts", "rep"), "tp", None),
        P(("parts", "rep"), "tp", None, None),
        P(("parts", "rep"), "tp", None, None, None),
        P(("parts", "rep"), None),
        P(("parts", "rep")),
        P(("parts", "rep"), None, None),
        P(("parts", "rep"), None, None),
        P(("parts", "rep"), None),
        P(("parts", "rep"), "tp"),
        P("tp", None),
        P(),
    )
    out_specs = P(("parts", "rep"), "tp")
    return jax.shard_map(
        on_device, mesh=mesh, in_specs=in_specs, out_specs=out_specs, check_vma=False
    )
```
